128 devices in a mesh: dp: 8 (over x_lo, y), tensor: 16 (over x_hi, z, core).
Axes of the slice: x: 4 (x_hi: 2, x_lo: 2; x = x_hi * 2 + x_lo), y: 4, z: 4, core: 2. Of those that a mesh axis runs over, the one named last changes fastest.
Arguments:
- hidden: bfloat16 [8, 512, 8192], P('dp'), may hold values from -70 to 70, as said below
- lengths: int32 [8], P('dp'), may hold values from 128 to 512, as said below
- norm_gain: float32 [8192], replicated, may hold values from 0.1 to 1.9
- w_q: float32 [8192, 8192], P(('dp', 'tensor')), may hold values from -1 to 1
- w_k: float32 [8192, 1024], P(('dp', 'tensor')), may hold values from -1 to 1
- w_v: float32 [8192, 1024], P(('dp', 'tensor')), may hold values from -1 to 1
- w_out: float32 [8192, 8192], P(('dp', 'tensor')), may hold values from -1 to 1
- b_q: float32 [8192], replicated, may hold values from -20 to 20
- b_k: float32 [1024], replicated, may hold values from -20 to 20
- b_v: float32 [1024], replicated, may hold values from -4 to 4
Outputs:
- layer_out: bfloat16 [8, 512, 8192], P('dp')
The draws below stay inside these ranges and needn't reach their ends.
Inputs may be any that keep to these rules, and one draw needn't show every extreme that they name: `hidden`: activations have row scales between 1 and 10. `lengths`: at least one replica has all 512 tokens live in every draw.
All inputs are finite; a program needn't handle non-finite values.
Results may differ from the reference program's by a relative error of at most 0.023.
Values may be sent and summed in bfloat16 or wider, within the bound.
A program may use at most 256 MiB of HBM per device.

```python
import math
import jax
import jax.numpy as jnp
from jax import lax

D = 8192
HQ = 64
KV = 8
HD = 128
TILE = 128
TOK = 512
N_DP = 8
N_TENSOR = 16


LOG_TEN = 2.302585


SQUARE_MEAN = 21.5


def spread_factors(key, count):
    return jnp.exp(jax.random.uniform(key, (count,), jnp.float32) * LOG_TEN)


def plant_outliers(key, weight, rows, cols):
    keys = jax.random.split(key, 3)
    tile_rows = rows // TILE
    tile_cols = cols // TILE
    shaped = weight.reshape(tile_rows, TILE, tile_cols, TILE)
    peaks = jnp.max(jnp.abs(shaped), axis=(1, 3))
    position_row = jax.random.randint(keys[0], (tile_rows, tile_cols), 0, TILE)
    position_col = jax.random.randint(keys[1], (tile_rows, tile_cols), 0, TILE)
    sign_pick = jax.random.randint(keys[2], (tile_rows, tile_cols), 0, 2)
    signed = jnp.where(sign_pick == 1, 1.0, -1.0).astype(jnp.float32)
    factor = max(1.0, min(16.0, TILE / 8.0))
    planted_value = signed * jnp.minimum(factor * peaks, 1.0)
    offsets = jnp.arange(TILE)
    chosen = (offsets[None, :, None, None] == position_row[:, None, :, None]) & (offsets[None, None, None, :] == position_col[:, None, :, None])
    planted = jnp.where(chosen, planted_value[:, None, :, None], shaped)
    return planted.reshape(rows, cols)


def scaled_weight(key, base, rows, cols, fan_in):
    keys = jax.random.split(key, 3)
    row_factor = spread_factors(keys[0], rows)
    col_factor = spread_factors(keys[1], cols)
    scaled = base * row_factor[:, None] * col_factor[None, :] / (SQUARE_MEAN * math.sqrt(fan_in))
    return plant_outliers(keys[2], scaled, rows, cols)


def weight_base(key, rows, cols):
    return jax.random.truncated_normal(key, -4.0, 4.0, (rows, cols), jnp.float32)


def draw_hidden(key, part):
    key = jax.random.fold_in(key, 3)
    keys = jax.random.split(key, 2)
    base = jax.random.truncated_normal(keys[0], -6.0, 6.0, (N_DP, TOK, D), jnp.float32)
    factor = spread_factors(keys[1], N_DP * TOK).reshape(N_DP, TOK, 1)
    return (base * factor).astype(jnp.bfloat16)


def draw_lengths(key, part):
    key = jax.random.fold_in(key, 5)
    keys = jax.random.split(key, 2)
    drawn = jax.random.randint(keys[0], (N_DP,), TOK // 4, TOK + 1)
    full = jax.random.randint(keys[1], (), 0, N_DP)
    return jnp.where(jnp.arange(N_DP) == full, TOK, drawn).astype(jnp.int32)


def draw_w_q(key, part):
    key = jax.random.fold_in(key, 7)
    keys = jax.random.split(key, 2)
    base = weight_base(keys[0], D, HQ * HD)
    return scaled_weight(keys[1], base, D, HQ * HD, D)


def draw_w_k(key, part):
    key = jax.random.fold_in(key, 11)
    keys = jax.random.split(key, 2)
    base = weight_base(keys[0], D, KV * HD)
    return scaled_weight(keys[1], base, D, KV * HD, D)


def draw_w_v(key, part):
    key = jax.random.fold_in(key, 13)
    keys = jax.random.split(key, 2)
    base = weight_base(keys[0], D, KV * HD)
    return scaled_weight(keys[1], base, D, KV * HD, D)


def draw_w_out(key, part):
    key = jax.random.fold_in(key, 17)
    keys = jax.random.split(key, 2)
    base = weight_base(keys[0], D, HQ * HD)
    return scaled_weight(keys[1], base, D, HQ * HD, HQ * HD)


def draw_b_k(key, part):
    key = jax.random.fold_in(key, 31)
    return 0.5 * jax.random.truncated_normal(key, -4.0, 4.0, (KV * HD,), jnp.float32)


def draw_b_q(key, part):
    key = jax.random.fold_in(key, 37)
    return 0.5 * jax.random.truncated_normal(key, -4.0, 4.0, (HQ * HD,), jnp.float32)


def normal_values(rng, shape, spread, reach, dtype=jnp.bfloat16):
    result = jax.random.normal(rng, shape, jnp.float32) * spread
    return jnp.minimum(jnp.maximum(result, -reach), reach).astype(dtype)


def setup_inputs(seed: int = 0) -> dict:
    seeds = jax.random.split(jax.random.key(seed), 11)
    hidden = draw_hidden(jax.random.fold_in(seeds[10], 71), 0)
    lengths = draw_lengths(jax.random.fold_in(seeds[10], 71), 0)
    norm_gain = jnp.clip(1.0 + 0.18 * jax.random.normal(seeds[2], (D,), jnp.float32), 0.1, 1.9)
    w_q = draw_w_q(jax.random.fold_in(seeds[10], 71), 0)
    w_k = draw_w_k(jax.random.fold_in(seeds[10], 71), 0)
    w_v = draw_w_v(jax.random.fold_in(seeds[10], 71), 0)
    w_out = draw_w_out(jax.random.fold_in(seeds[10], 71), 0)
    b_q = draw_b_q(jax.random.fold_in(seeds[10], 71), 0)
    b_k = draw_b_k(jax.random.fold_in(seeds[10], 71), 0)
    b_v = normal_values(seeds[9], (KV * HD,), 0.5, 4.0, jnp.float32)
    return {"hidden": hidden, "lengths": lengths, "norm_gain": norm_gain, "w_q": w_q, "w_k": w_k, "w_v": w_v, "w_out": w_out, "b_q": b_q, "b_k": b_k, "b_v": b_v}


THETA = 1000000.0
NORM_EPS = 1e-06
PEAK_EPS = 1e-06
LEVEL_TOP = 127.0

def tile_quant(weight):
    rows, cols = weight.shape
    shaped = weight.reshape(rows // TILE, TILE, cols // TILE, TILE)
    peaks = lax.optimization_barrier(jnp.max(jnp.abs(shaped), axis=(1, 3)))
    scales = lax.optimization_barrier(((peaks + PEAK_EPS) / LEVEL_TOP).astype(jnp.bfloat16)).astype(jnp.float32)
    levels = jnp.floor(shaped / scales[:, None, :, None] + 0.5)
    return (levels * scales[:, None, :, None]).astype(jnp.bfloat16).reshape(rows, cols)

def rotary(values, count, tokens):
    positions = jnp.arange(tokens).astype(jnp.float32)
    freqs = THETA ** (-jnp.arange(0, HD, 2).astype(jnp.float32) / HD)
    angles = positions[:, None] * freqs[None, :]
    cosine = jnp.cos(angles)[:, None, :]
    sine = jnp.sin(angles)[:, None, :]
    shaped = values.reshape(tokens, count, HD)
    first = shaped[:, :, :HD // 2]
    second = shaped[:, :, HD // 2:]
    return jnp.concatenate((first * cosine - second * sine, second * cosine + first * sine), axis=2)

def attention(query, keys, values, length, heads, kv_heads):
    tokens = query.shape[0]
    group = heads // kv_heads
    grouped = query.reshape(tokens, kv_heads, group, HD).astype(jnp.float32)
    scores = jnp.einsum('qkgd,skd->kgqs', grouped, keys.astype(jnp.float32)) * HD ** (-0.5)
    rows = jnp.arange(tokens)[:, None]
    cols = jnp.arange(tokens)[None, :]
    keep = (cols <= rows) & (cols < length)
    scores = jnp.where(keep[None, None], scores, -1e+30)
    peak = lax.optimization_barrier(jnp.max(scores, axis=3, keepdims=True))
    expo = jnp.exp(scores - peak)
    probs = (expo / lax.optimization_barrier(jnp.sum(expo, axis=3, keepdims=True))).astype(jnp.bfloat16)
    mixed = jnp.einsum('kgqs,skd->qkgd', probs.astype(jnp.float32), values.astype(jnp.float32))
    return mixed.astype(jnp.bfloat16).reshape(tokens, heads * HD)

def reference(hidden, lengths, norm_gain, w_q, w_k, w_v, w_out, b_q, b_k, b_v):
    wq = tile_quant(w_q)
    wk = tile_quant(w_k)
    wv = tile_quant(w_v)
    wo = tile_quant(w_out)
    head_cols = HQ * HD // N_TENSOR

    def replica(item):
        rows, length = item
        tokens = rows.shape[0]
        wide = rows.astype(jnp.float32)
        normed = (wide * lax.rsqrt(lax.optimization_barrier(jnp.mean(wide * wide, axis=1, keepdims=True)) + NORM_EPS) * norm_gain).astype(jnp.bfloat16)
        query = jnp.dot(normed, wq, preferred_element_type=jnp.float32) + b_q
        keys = jnp.dot(normed, wk, preferred_element_type=jnp.float32) + b_k
        values = jnp.dot(normed, wv, preferred_element_type=jnp.float32) + b_v
        query = rotary(query, HQ, tokens).astype(jnp.bfloat16)
        keys = rotary(keys, KV, tokens).astype(jnp.bfloat16)
        values = values.reshape(tokens, KV, HD).astype(jnp.bfloat16)
        attended = attention(query, keys, values, length, HQ, KV)
        parts = jnp.einsum('tgc,egc->gte', attended.reshape(tokens, N_TENSOR, head_cols).astype(jnp.float32), wo.reshape(D, N_TENSOR, head_cols).astype(jnp.float32))
        rounded = lax.optimization_barrier(parts.astype(jnp.bfloat16)).astype(jnp.float32)
        return lax.optimization_barrier(jnp.sum(rounded, axis=0)).astype(jnp.bfloat16)
    return lax.map(replica, (hidden, lengths))
```

```python
import functools

import jax
import jax.numpy as jnp
from jax import lax
from jax.experimental import pallas as pl
from jax.experimental.pallas import tpu as pltpu
from jax.sharding import PartitionSpec as P

D = 8192
HQ = 64
KV = 8
HD = 128
TILE = 128
TOK = 512
GROUPS = 16
GCOLS = 512
WCOLS = 640
ROWS = 64
THETA = 1000000.0
NORM_EPS = 1e-06
PEAK_EPS = 1e-06
LEVEL_TOP = 127.0
MESH = pl.DeviceIdType.MESH
QT = 64
KT = 8


def kernel(
    len_ref, hid_hbm, gain, wq, wk, wv, wo, bq, bk, bv, cos, sin, out,
    wf, pm, pk_own, pk_oth, sc, hid, send_a, wbuf, send_o, wobuf, acc, qb, kv_own, kv_oth, att, acc2, outb,
    ld_sem, pk_sem, a_send, a_recv, b_send, b_recv, sib_sem, o_send, o_recv, kv_sem, t_send, t_recv, g_send, g_recv, g_loc,
):
    dp = lax.axis_index("dp")
    t = lax.axis_index("tensor")
    xl, y = dp // 4, dp % 4
    xh, z, c = t // 8, (t // 2) % 4, t % 2

    def dev(xl_, y_, xh_, z_, c_):
        return (xl_ * 4 + y_, xh_ * 8 + z_ * 2 + c_)

    y_up, y_dn, y_op = (y + 1) % 4, (y + 3) % 4, (y + 2) % 4
    z_up, z_dn, z_op = (z + 1) % 4, (z + 3) % 4, (z + 2) % 4
    dev_yu, dev_yd = dev(xl, y_up, xh, z, c), dev(xl, y_dn, xh, z, c)
    dev_xp = dev(1 - xl, y, (xh + c) % 2, z, c)
    dev_zu, dev_zd = dev(xl, y, xh, z_up, c), dev(xl, y, xh, z_dn, c)
    dev_xh = dev(xl, y, 1 - xh, z, c)
    dev_sib = dev(xl, y, xh, z, 1 - c)
    dev_kv = dev(xl, y, (xh + xl) % 2, z, 1 - c)

    def group_of(t_):
        return ((t_ // 8 + (t_ % 2) * xl) % 2) * 8 + t_ % 8

    def remote(src, dst, ss, rs, device):
        return pltpu.make_async_remote_copy(
            src_ref=src, dst_ref=dst, send_sem=ss, recv_sem=rs, device_id=device, device_id_type=MESH
        )

    loads = (
        pltpu.make_async_copy(wq, wf.at[:, 0:8192], ld_sem.at[0]),
        pltpu.make_async_copy(wk, wf.at[:, 8192:9216], ld_sem.at[1]),
        pltpu.make_async_copy(wv, wf.at[:, 9216:10240], ld_sem.at[2]),
        pltpu.make_async_copy(wo, wf.at[:, 10240:18432], ld_sem.at[3]),
        pltpu.make_async_copy(hid_hbm, hid, ld_sem.at[4]),
    )
    for cp in loads:
        cp.start()

    barrier = pltpu.get_barrier_semaphore()

    @pl.loop(1, 16)
    def _(i):
        pl.semaphore_signal(barrier, inc=1, device_id=(dp, (t + i) % 16), device_id_type=MESH)

    for peer in (dev_yu, dev_yd, dev_xp):
        pl.semaphore_signal(barrier, inc=1, device_id=peer, device_id_type=MESH)

    for cp in loads[:4]:
        cp.wait()

    @pl.loop(0, 144, unroll=4)
    def _(j):
        tile = jnp.abs(wf[:, pl.ds(pl.multiple_of(j * 128, 128), 128)])
        pm[j] = jnp.max(tile.reshape(8, 8, 128), axis=0)

    peaks = jnp.max(jnp.max(pm[...], axis=1), axis=1, keepdims=True)
    pk_own[...] = jnp.broadcast_to(peaks, (144, 128))

    pl.semaphore_wait(barrier, 18)
    swap = remote(pk_own, pk_oth, pk_sem.at[0], pk_sem.at[1], dev_sib)
    swap.start()
    swap.wait()
    full = jnp.maximum(pk_own[...], pk_oth[...])
    sc[...] = ((full + PEAK_EPS) / LEVEL_TOP).astype(jnp.bfloat16).astype(jnp.float32)

    def quantized(j):
        tile = wf[:, pl.ds(pl.multiple_of(j * 128, 128), 128)]
        s = sc[pl.ds(j, 1), :]
        return (jnp.floor(tile / s + 0.5) * s).astype(jnp.bfloat16)

    my_rows = pl.ds(pl.multiple_of(dp * 1024 + t * 64, 64), 64)

    @pl.loop(0, 16)
    def _(i):
        to = (t + i) % 16
        g = group_of(to)
        for n in range(4):
            send_a[g, :, n * 128 : (n + 1) * 128] = quantized(g * 4 + n)
        send_a[g, :, 512:640] = quantized(QT + KT * (to % 2) + g // 2)

        @pl.when(i == 0)
        def _():
            pltpu.make_async_copy(send_a.at[g], wbuf.at[my_rows], a_recv.at[t]).start()

        @pl.when(i > 0)
        def _():
            remote(send_a.at[g], wbuf.at[my_rows], a_send.at[to], a_recv.at[t], (dp, to)).start()

    source = y % 2 == c
    slot = y // 2

    @pl.loop(0, 64)
    def _(j):
        send_o[:, pl.ds(pl.multiple_of(j * 128, 128), 128)] = quantized(QT + 2 * KT + j)

    half_rows = pl.ds(pl.multiple_of((y // 2) * 128 + c * 64, 64), 64)

    @pl.when(source)
    def _():
        pltpu.make_async_copy(send_o, wobuf.at[half_rows], sib_sem.at[0]).start()

    @pl.when(jnp.logical_not(source))
    def _():
        remote(send_o, wobuf.at[half_rows], sib_sem.at[1], sib_sem.at[2], dev_sib).start()

    loads[4].wait()

    @pl.loop(0, 32)
    def _(i):
        rows = pl.ds(pl.multiple_of(i * 16, 16), 16)
        wide = hid[rows, :].astype(jnp.float32)
        ms = jnp.mean(wide * wide, axis=1, keepdims=True)
        hid[rows, :] = (wide * lax.rsqrt(ms + NORM_EPS) * gain[...]).astype(jnp.bfloat16)

    def b_rows(xl_, y_, k):
        return pl.ds(pl.multiple_of((xl_ * 4 + y_) * 1024 + k * 256, 256), 256)

    def b_copy(y_, k, n, side, device):
        ref = wbuf.at[b_rows(xl, y_, k)]
        return remote(ref, ref, b_send.at[n], b_recv.at[side, y_, k], device)

    def b_wait(side, y_, k):
        xs = xl if side == 0 else 1 - xl
        ref = wbuf.at[b_rows(xs, y_, k)]
        remote(ref, ref, b_send.at[0], b_recv.at[side, y_, k], dev_xp).wait_recv()

    def project(xl_, y_, first=False):
        base = (xl_ * 4 + y_) * 1024
        for n in range(2):
            cols = pl.ds(pl.multiple_of(base + n * 512, 512), 512)
            part = jnp.dot(hid[:, cols], wbuf[cols, :], preferred_element_type=jnp.float32)
            if first and n == 0:
                acc[...] = part
            else:
                acc[...] += part

    @pl.loop(0, 4)
    def _(k):
        @pl.loop(0, 4)
        def _(n):
            src_t = k * 4 + n
            rows = pl.ds(pl.multiple_of(dp * 1024 + src_t * 64, 64), 64)
            ref = wbuf.at[rows]
            remote(ref, ref, a_send.at[0], a_recv.at[src_t], dev_xp).wait_recv()

        b_copy(y, k, 7 * k, 0, dev_yu).start()
        b_copy(y, k, 7 * k + 1, 0, dev_yd).start()
        b_copy(y, k, 7 * k + 2, 1, dev_xp).start()

    @pl.loop(0, 4)
    def _(k):
        b_wait(0, y_dn, k)
        b_copy(y_dn, k, 7 * k + 3, 1, dev_xp).start()

        @pl.when(k < 2)
        def _():
            b_copy(y_dn, k, 7 * k + 4, 0, dev_yu).start()

        b_wait(0, y_up, k)
        b_copy(y_up, k, 7 * k + 5, 1, dev_xp).start()

        @pl.when(k >= 2)
        def _():
            b_copy(y_up, k, 7 * k + 4, 0, dev_yd).start()

    project(xl, y, first=True)

    @pl.loop(0, 4)
    def _(k):
        b_wait(0, y_op, k)
        b_copy(y_op, k, 7 * k + 6, 1, dev_xp).start()

    def o_rows(side, s, k):
        return pl.ds(pl.multiple_of(side * 256 + s * 128 + k * 32, 32), 32)

    def o_copy(s, k, n, side, device):
        return remote(
            wobuf.at[o_rows(0, s, k)], wobuf.at[o_rows(side, s, k)], o_send.at[n], o_recv.at[side, s, k], device
        )

    def o_wait(side, s, k):
        ref = wobuf.at[o_rows(side, s, k)]
        remote(ref, ref, o_send.at[0], o_recv.at[side, s, k], dev_xp).wait_recv()

    @pl.when(source)
    def _():
        pltpu.make_async_copy(send_o, wobuf.at[half_rows], sib_sem.at[0]).wait()
        remote(send_o, wobuf.at[half_rows], sib_sem.at[1], sib_sem.at[2], dev_sib).wait_recv()

        @pl.loop(0, 4)
        def _(k):
            o_copy(slot, k, 4 * k, 0, dev_yu).start()
            o_copy(slot, k, 4 * k + 1, 0, dev_yd).start()
            o_copy(slot, k, 4 * k + 2, 1, dev_xp).start()

    @pl.loop(1, 4)
    def _(n):
        project(xl, (y + n) % 4)

    @pl.loop(0, 4)
    def _(n):
        src_y = (y + jnp.where(n == 1, 3, jnp.where(n == 2, 1, jnp.where(n == 3, 2, 0)))) % 4

        @pl.loop(0, 4)
        def _(k):
            b_wait(1, src_y, k)

        project(1 - xl, src_y)

    g_me = group_of(t)

    def rotated(x):
        return x * cos[...] + pltpu.roll(x, 64, 1) * sin[...]

    bias_kv = jnp.where(c == 0, bk[pl.ds(g_me // 2, 1), :], bv[pl.ds(g_me // 2, 1), :])
    raw = acc[:, 512:640] + bias_kv
    kv_own[...] = jnp.where(c == 0, rotated(raw), raw).astype(jnp.bfloat16)
    kv_swap = remote(kv_own, kv_oth, kv_sem.at[0], kv_sem.at[1], dev_kv)
    kv_swap.start()

    for h in range(4):
        cols = slice(h * 128, (h + 1) * 128)
        raw_q = acc[:, cols] + bq[pl.ds(g_me * 4 + h, 1), :]
        qb[:, cols] = rotated(raw_q).astype(jnp.bfloat16)

    @pl.when(jnp.logical_not(source))
    def _():
        s_dn, s_up = y_dn // 2, y_up // 2

        @pl.loop(0, 4)
        def _(k):
            o_wait(0, s_dn, k)
            o_copy(s_dn, k, 4 * k, 1, dev_xp).start()

            @pl.when(k < 2)
            def _():
                o_copy(s_dn, k, 4 * k + 1, 0, dev_yu).start()

            o_wait(0, s_up, k)
            o_copy(s_up, k, 4 * k + 2, 1, dev_xp).start()

            @pl.when(k >= 2)
            def _():
                o_copy(s_up, k, 4 * k + 1, 0, dev_yd).start()

    kv_swap.wait()
    keys = jnp.where(c == 0, kv_own[...], kv_oth[...])
    values = jnp.where(c == 0, kv_oth[...], kv_own[...])
    kv_own[...] = keys
    kv_oth[...] = values

    length = len_ref[0]

    @pl.loop(0, 4)
    def _(h):
        cols = pl.ds(pl.multiple_of(h * 128, 128), 128)
        for n in range(2):
            lo, hi = n * 256, (n + 1) * 256
            s = lax.dot_general(
                qb[lo:hi, cols], kv_own[0:hi, :], (((1,), (1,)), ((), ())), preferred_element_type=jnp.float32
            ) * HD ** (-0.5)
            r = lax.broadcasted_iota(jnp.int32, (256, hi), 0) + lo
            k = lax.broadcasted_iota(jnp.int32, (256, hi), 1)
            s = jnp.where((k <= r) & (k < length), s, -1e30)
            e = jnp.exp(s - jnp.max(s, axis=1, keepdims=True))
            p = (e / jnp.sum(e, axis=1, keepdims=True)).astype(jnp.bfloat16)
            o = jnp.dot(p, kv_oth[0:hi, :], preferred_element_type=jnp.float32)
            att[g_me, lo:hi, cols] = o.astype(jnp.bfloat16)

    def t_ref(src_t, h):
        return att.at[group_of(src_t), pl.ds(pl.multiple_of(h * 256, 256), 256)]

    def t_copy(src_t, h, n, device):
        ref = t_ref(src_t, h)
        return remote(ref, ref, t_send.at[n], t_recv.at[src_t, h], device)

    def t_wait(src_t, h):
        ref = t_ref(src_t, h)
        remote(ref, ref, t_send.at[0], t_recv.at[src_t, h], dev_sib).wait_recv()

    def tid(xh_, z_, c_):
        return xh_ * 8 + z_ * 2 + c_

    def plane_gather(copy, wait, chunks, own_started):
        low = chunks // 2
        if not own_started:

            @pl.loop(0, chunks)
            def _(h):
                start_own(copy, h)

        for s in range(2):
            xs = xh if s == 0 else 1 - xh
            if s == 1:

                @pl.loop(0, chunks)
                def _(h):
                    src = tid(xs, z, c)
                    wait(src, h)
                    copy(src, h, 15 * h + 4, dev_zu).start()
                    copy(src, h, 15 * h + 5, dev_zd).start()
                    copy(src, h, 15 * h + 6, dev_sib).start()

            @pl.loop(0, chunks)
            def _(h):
                dn, up = tid(xs, z_dn, c), tid(xs, z_up, c)
                wait(dn, h)

                @pl.when(h < low)
                def _():
                    copy(dn, h, 15 * h + 7 + 4 * s, dev_zu).start()

                copy(dn, h, 15 * h + 8 + 4 * s, dev_sib).start()
                wait(up, h)

                @pl.when(h >= low)
                def _():
                    copy(up, h, 15 * h + 7 + 4 * s, dev_zd).start()

                copy(up, h, 15 * h + 9 + 4 * s, dev_sib).start()

        for s in range(2):
            xs = xh if s == 0 else 1 - xh

            @pl.loop(0, chunks)
            def _(h):
                op = tid(xs, z_op, c)
                wait(op, h)
                copy(op, h, 15 * h + 10 + 4 * s, dev_sib).start()

    def start_own(copy, h):
        copy(t, h, 15 * h, dev_xh).start()
        copy(t, h, 15 * h + 1, dev_zu).start()
        copy(t, h, 15 * h + 2, dev_zd).start()
        copy(t, h, 15 * h + 3, dev_sib).start()

    def wait_sibling(wait, chunks):
        @pl.loop(0, 8)
        def _(n):
            @pl.loop(0, chunks)
            def _(h):
                wait(n * 2 + 1 - c, h)

    @pl.loop(0, 2)
    def _(h):
        start_own(t_copy, h)

    @pl.when(source)
    def _():
        @pl.loop(0, 4)
        def _(k):
            o_wait(0, 1 - slot, k)
            o_copy(1 - slot, k, 4 * k + 3, 1, dev_xp).start()

    plane_gather(t_copy, t_wait, 2, True)
    wait_sibling(t_wait, 2)

    @pl.loop(0, 4)
    def _(k):
        o_wait(1, 0, k)
        o_wait(1, 1, k)

    def out_block(src_t, j):
        xh_s, z_s, c_s = src_t // 8, (src_t // 2) % 4, src_t % 2
        side, s = j // 2, j % 2
        xl_b = (xl + side) % 2
        xh_b = (xh_s + side * c_s) % 2
        return (xl_b * 4 + c_s + 2 * s) * 8 + xh_b * 4 + z_s

    def g_ref(src_t, j):
        return out.at[:, pl.ds(pl.multiple_of(out_block(src_t, j) * 128, 128), 128)]

    def g_copy_own(src_t, j, n, device):
        return remote(outb.at[j], g_ref(src_t, j), g_send.at[n], g_recv.at[src_t, j], device)

    def g_copy(src_t, j, n, device):
        ref = g_ref(src_t, j)
        return remote(ref, ref, g_send.at[n], g_recv.at[src_t, j], device)

    def g_wait(src_t, j):
        ref = g_ref(src_t, j)
        remote(ref, ref, g_send.at[0], g_recv.at[src_t, j], dev_sib).wait_recv()

    for half in range(2):

        @pl.loop(0, 16)
        def _(g):
            part = lax.dot_general(
                att[g],
                wobuf[half * 256 : (half + 1) * 256, pl.ds(pl.multiple_of(g * 512, 512), 512)],
                (((1,), (1,)), ((), ())),
                preferred_element_type=jnp.float32,
            )
            acc2[...] = jnp.where(g == 0, part, acc2[...] + part)

        for n in range(2):
            j = half * 2 + n
            outb[j] = acc2[:, n * 128 : (n + 1) * 128].astype(jnp.bfloat16)
            pltpu.make_async_copy(outb.at[j], g_ref(t, j), g_loc.at[j]).start()
            start_own(g_copy_own, j)

    plane_gather(g_copy, g_wait, 4, True)
    wait_sibling(g_wait, 4)

    for j in range(4):
        pltpu.make_async_copy(outb.at[j], g_ref(t, j), g_loc.at[j]).wait()

    def drain(ref, sem):
        remote(ref, ref, sem, sem, dev_sib).wait_send()

    @pl.loop(1, 16)
    def _(i):
        drain(send_a.at[0], a_send.at[(t + i) % 16])

    @pl.when(jnp.logical_not(source))
    def _():
        drain(send_o, sib_sem.at[1])

    @pl.loop(0, 28)
    def _(n):
        drain(wbuf.at[0:256], b_send.at[n])

    @pl.loop(0, 4)
    def _(k):
        for n in range(3):
            drain(wobuf.at[0:32], o_send.at[4 * k + n])

        @pl.when(source)
        def _():
            drain(wobuf.at[0:32], o_send.at[4 * k + 3])

    @pl.loop(0, 30)
    def _(n):
        drain(att.at[0, 0:256], t_send.at[n])

    @pl.loop(0, 60)
    def _(n):
        drain(outb.at[0], g_send.at[n])


def local(hidden, lengths, norm_gain, w_q, w_k, w_v, w_out, b_q, b_k, b_v):
    positions = jnp.arange(TOK).astype(jnp.float32)
    freqs = THETA ** (-jnp.arange(0, HD, 2).astype(jnp.float32) / HD)
    angles = positions[:, None] * freqs[None, :]
    cosine, sine = jnp.cos(angles), jnp.sin(angles)
    cos = jnp.concatenate((cosine, cosine), axis=1)
    sin = jnp.concatenate((-sine, sine), axis=1)
    anywhere = pl.BlockSpec(memory_space=pl.ANY)
    vmem = pl.BlockSpec(memory_space=pltpu.VMEM)
    bf, f32 = jnp.bfloat16, jnp.float32
    dma = pltpu.SemaphoreType.DMA
    result = pl.pallas_call(
        kernel,
        out_shape=jax.ShapeDtypeStruct((TOK, D), bf),
        in_specs=[pl.BlockSpec(memory_space=pltpu.SMEM), anywhere, vmem]
        + [anywhere] * 4
        + [vmem] * 5,
        out_specs=anywhere,
        scratch_shapes=[
            pltpu.VMEM((ROWS, 18432), f32),
            pltpu.VMEM((144, 8, 128), f32),
            pltpu.VMEM((144, 128), f32),
            pltpu.VMEM((144, 128), f32),
            pltpu.VMEM((144, 128), f32),
            pltpu.VMEM((TOK, D), bf),
            pltpu.VMEM((GROUPS, ROWS, WCOLS), bf),
            pltpu.VMEM((D, WCOLS), bf),
            pltpu.VMEM((ROWS, D), bf),
            pltpu.VMEM((512, D), bf),
            pltpu.VMEM((TOK, WCOLS), f32),
            pltpu.VMEM((TOK, GCOLS), bf),
            pltpu.VMEM((TOK, HD), bf),
            pltpu.VMEM((TOK, HD), bf),
            pltpu.VMEM((GROUPS, TOK, GCOLS), bf),
            pltpu.VMEM((TOK, 256), f32),
            pltpu.VMEM((4, TOK, 128), bf),
            dma((5,)),
            dma((2,)),
            dma((16,)),
            dma((16,)),
            dma((28,)),
            dma((2, 4, 4)),
            dma((3,)),
            dma((16,)),
            dma((2, 2, 4)),
            dma((2,)),
            dma((30,)),
            dma((16, 2)),
            dma((60,)),
            dma((16, 4)),
            dma((4,)),
        ],
        compiler_params=pltpu.CompilerParams(
            collective_id=0, has_side_effects=True, vmem_limit_bytes=62 * 2**20
        ),
    )(
        lengths, hidden[0], norm_gain.reshape(1, D), w_q, w_k, w_v, w_out,
        b_q.reshape(HQ, HD), b_k.reshape(KV, HD), b_v.reshape(KV, HD), cos, sin,
    )
    return result[None]


def solution(mesh):
    rows = P(("dp", "tensor"), None)
    placed = (P("dp", None, None), P("dp"), P(), rows, rows, rows, rows, P(), P(), P())
    return jax.shard_map(
        local, mesh=mesh, in_specs=placed, out_specs=P("dp", None, None), check_vma=False
    )
```

```python
import functools

import jax
import jax.numpy as jnp
import numpy as np
from jax import lax
from jax.experimental import pallas as pl
from jax.experimental.pallas import tpu as pltpu
from jax.sharding import PartitionSpec as P

D = 8192
HQ = 64
KV = 8
HD = 128
TILE = 128
TOK = 512
GROUPS = 16
GCOLS = 512
WCOLS = 640
ROWS = 64
THETA = 1000000.0
NORM_EPS = 1e-06
PEAK_EPS = 1e-06
LEVEL_TOP = 127.0
MESH = pl.DeviceIdType.MESH
QT = 64
KT = 8
Q_CHUNKS = 8
Q_FIRST = 3
O_CHUNKS = 4
O_FIRST = 2
G_FIRST = 2


def kernel(
    len_ref, hid_hbm, gain, wq, wk, wv, wo, bq, bk, bv, cos, sin, out,
    wf, pm, pk_own, pk_oth, sc, hid, send_a, wbuf, send_o, wobuf, acc, qb, kv_own, kv_oth, att, acc2, outb,
    ld_sem, pk_sem, a_send, a_recv, b_send, b_recv, sib_sem, o_send, o_recv, kv_sem, t_send, t_recv, g_send, g_recv, g_loc,
):
    dp = lax.axis_index("dp")
    t = lax.axis_index("tensor")
    xl, y = dp // 4, dp % 4
    xh, z, c = t // 8, (t // 2) % 4, t % 2

    def dev(xl_, y_, xh_, z_, c_):
        return (xl_ * 4 + y_, xh_ * 8 + z_ * 2 + c_)

    y_up, y_dn, y_op = (y + 1) % 4, (y + 3) % 4, (y + 2) % 4
    z_up, z_dn, z_op = (z + 1) % 4, (z + 3) % 4, (z + 2) % 4
    dev_yu, dev_yd = dev(xl, y_up, xh, z, c), dev(xl, y_dn, xh, z, c)
    dev_xp = dev(1 - xl, y, (xh + c) % 2, z, c)
    dev_zu, dev_zd = dev(xl, y, xh, z_up, c), dev(xl, y, xh, z_dn, c)
    dev_xh = dev(xl, y, 1 - xh, z, c)
    dev_sib = dev(xl, y, xh, z, 1 - c)
    dev_kv = dev(xl, y, (xh + xl) % 2, z, 1 - c)

    def group_of(t_):
        return ((t_ // 8 + (t_ % 2) * xl) % 2) * 8 + t_ % 8

    def remote(src, dst, ss, rs, device):
        return pltpu.make_async_remote_copy(
            src_ref=src, dst_ref=dst, send_sem=ss, recv_sem=rs, device_id=device, device_id_type=MESH
        )

    loads = (
        pltpu.make_async_copy(wq, wf.at[:, 0:8192], ld_sem.at[0]),
        pltpu.make_async_copy(wk, wf.at[:, 8192:9216], ld_sem.at[1]),
        pltpu.make_async_copy(wv, wf.at[:, 9216:10240], ld_sem.at[2]),
        pltpu.make_async_copy(wo, wf.at[:, 10240:18432], ld_sem.at[3]),
        pltpu.make_async_copy(hid_hbm, hid, ld_sem.at[4]),
    )
    for cp in loads:
        cp.start()

    barrier = pltpu.get_barrier_semaphore()

    @pl.loop(1, 16)
    def _(i):
        pl.semaphore_signal(barrier, inc=1, device_id=(dp, (t + i) % 16), device_id_type=MESH)

    for peer in (dev_yu, dev_yd, dev_xp):
        pl.semaphore_signal(barrier, inc=1, device_id=peer, device_id_type=MESH)

    for cp in loads[:4]:
        cp.wait()

    @pl.loop(0, 144, unroll=4)
    def _(j):
        tile = jnp.abs(wf[:, pl.ds(pl.multiple_of(j * 128, 128), 128)])
        pm[j] = jnp.max(tile.reshape(8, 8, 128), axis=0)

    peaks = jnp.max(jnp.max(pm[...], axis=1), axis=1, keepdims=True)
    pk_own[...] = jnp.broadcast_to(peaks, (144, 128))

    pl.semaphore_wait(barrier, 18)
    swap = remote(pk_own, pk_oth, pk_sem.at[0], pk_sem.at[1], dev_sib)
    swap.start()
    swap.wait()
    full = jnp.maximum(pk_own[...], pk_oth[...])
    sc[...] = ((full + PEAK_EPS) / LEVEL_TOP).astype(jnp.bfloat16).astype(jnp.float32)

    def quantized(j):
        tile = wf[:, pl.ds(pl.multiple_of(j * 128, 128), 128)]
        s = sc[pl.ds(j, 1), :]
        return (jnp.floor(tile / s + 0.5) * s).astype(jnp.bfloat16)

    my_rows = pl.ds(pl.multiple_of(dp * 1024 + t * 64, 64), 64)

    hx = (xh + c * xl) % 2

    def ring(step):
        return jnp.where(step == 1, 3, jnp.where(step == 2, 1, jnp.where(step == 3, 2, 0)))

    @pl.loop(0, 16)
    def _(i):
        to_c = i % 2
        to = ((xh + i // 8 + to_c * xl) % 2) * 8 + ((z + 4 - ring((i // 2) % 4)) % 4) * 2 + to_c
        g = group_of(to)
        for n in range(4):
            send_a[g, :, n * 128 : (n + 1) * 128] = quantized(g * 4 + n)
        send_a[g, :, 512:640] = quantized(QT + KT * to_c + g // 2)

        @pl.when(to == t)
        def _():
            pltpu.make_async_copy(send_a.at[g], wbuf.at[my_rows], a_recv.at[t]).start()

        @pl.when(to != t)
        def _():
            remote(send_a.at[g], wbuf.at[my_rows], a_send.at[to], a_recv.at[t], (dp, to)).start()

    source = y % 2 == c
    slot = y // 2

    @pl.loop(0, 64)
    def _(j):
        send_o[:, pl.ds(pl.multiple_of(j * 128, 128), 128)] = quantized(QT + 2 * KT + j)

    half_rows = pl.ds(pl.multiple_of((y // 2) * 128 + c * 64, 64), 64)

    @pl.when(source)
    def _():
        pltpu.make_async_copy(send_o, wobuf.at[half_rows], sib_sem.at[0]).start()

    @pl.when(jnp.logical_not(source))
    def _():
        remote(send_o, wobuf.at[half_rows], sib_sem.at[1], sib_sem.at[2], dev_sib).start()

    loads[4].wait()

    @pl.loop(0, 32)
    def _(i):
        rows = pl.ds(pl.multiple_of(i * 16, 16), 16)
        wide = hid[rows, :].astype(jnp.float32)
        ms = jnp.mean(wide * wide, axis=1, keepdims=True)
        hid[rows, :] = (wide * lax.rsqrt(ms + NORM_EPS) * gain[...]).astype(jnp.bfloat16)

    def o_rows(side, s, k):
        return pl.ds(pl.multiple_of(side * 256 + s * 128 + k * 32, 32), 32)

    def o_copy(side, s, k, n, device, to_side):
        return remote(
            wobuf.at[o_rows(side, s, k)], wobuf.at[o_rows(to_side, s, k)], o_send.at[n],
            o_recv.at[to_side, s, k], device,
        )

    def o_wait(side, s, k):
        ref = wobuf.at[o_rows(side, s, k)]
        remote(ref, ref, o_send.at[0], o_recv.at[side, s, k], dev_xp).wait_recv()

    s_dn, s_up = y_dn // 2, y_up // 2

    def o_forward(side, k, n):
        @pl.when(k % 2 == 0)
        def _():
            o_copy(side, s_dn, k, n, dev_yu, side).start()

        @pl.when(k % 2 == 1)
        def _():
            o_copy(side, s_up, k, n, dev_yd, side).start()

    def b_chip(j):
        return ((hx + j // 4) % 2) * 4 + (z + ring(j % 4)) % 4

    def b_rows(side, y_, j):
        return pl.ds(pl.multiple_of((((xl + side) % 2) * 4 + y_) * 1024 + b_chip(j) * 128, 128), 128)

    def b_copy(side, y_, j, n, device, to_side):
        ref = wbuf.at[b_rows(side, y_, j)]
        return remote(ref, ref, b_send.at[n], b_recv.at[to_side, y_, j], device)

    def b_wait(side, y_, j):
        ref = wbuf.at[b_rows(side, y_, j)]
        remote(ref, ref, b_send.at[0], b_recv.at[side, y_, j], dev_xp).wait_recv()

    def b_forward(side, j, n):
        @pl.when(j % 2 == 0)
        def _():
            b_copy(side, y_dn, j, n, dev_yu, side).start()

        @pl.when(j % 2 == 1)
        def _():
            b_copy(side, y_up, j, n, dev_yd, side).start()

    def project(side, y_, first=False):
        base = (((xl + side) % 2) * 4 + y_) * 1024
        for n in range(2):
            cols = pl.ds(pl.multiple_of(base + n * 512, 512), 512)
            part = jnp.dot(hid[:, cols], wbuf[cols, :], preferred_element_type=jnp.float32)
            if first and n == 0:
                acc[...] = part
            else:
                acc[...] += part

    @pl.loop(0, Q_CHUNKS)
    def _(j):
        @pl.loop(0, 2)
        def _(n):
            src_t = b_chip(j) * 2 + n
            rows = pl.ds(pl.multiple_of(dp * 1024 + src_t * 64, 64), 64)
            ref = wbuf.at[rows]
            remote(ref, ref, a_send.at[0], a_recv.at[src_t], dev_xp).wait_recv()

        b_copy(0, y, j, 3 * j, dev_xp, 1).start()
        b_copy(0, y, j, 3 * j + 1, dev_yu, 0).start()
        b_copy(0, y, j, 3 * j + 2, dev_yd, 0).start()

    @pl.when(source)
    def _():
        pltpu.make_async_copy(send_o, wobuf.at[half_rows], sib_sem.at[0]).wait()
        remote(send_o, wobuf.at[half_rows], sib_sem.at[1], sib_sem.at[2], dev_sib).wait_recv()

        @pl.loop(0, O_FIRST)
        def _(k):
            o_copy(0, slot, k, 4 * k + 2, dev_xp, 1).start()

    @pl.loop(0, Q_FIRST)
    def _(j):
        n = 24 + 4 * j
        b_wait(1, y, j)
        b_copy(1, y, j, n, dev_yu, 1).start()
        b_copy(1, y, j, n + 1, dev_yd, 1).start()
        b_wait(0, y_dn, j)
        b_wait(0, y_up, j)
        b_forward(0, j, n + 2)

    @pl.loop(Q_FIRST, Q_CHUNKS)
    def _(j):
        n = 24 + 4 * j
        b_wait(0, y_dn, j)
        b_copy(0, y_dn, j, n, dev_xp, 1).start()
        b_wait(0, y_up, j)
        b_copy(0, y_up, j, n + 1, dev_xp, 1).start()
        b_forward(0, j, n + 2)

    @pl.loop(0, Q_FIRST)
    def _(j):
        b_wait(1, y_dn, j)
        b_wait(1, y_up, j)
        b_forward(1, j, 24 + 4 * j + 3)

    project(0, y, first=True)

    @pl.loop(Q_FIRST, Q_CHUNKS)
    def _(j):
        b_wait(0, y_op, j)
        b_copy(0, y_op, j, 24 + 4 * j + 3, dev_xp, 1).start()

    @pl.when(source)
    def _():
        @pl.loop(0, O_CHUNKS)
        def _(k):
            o_copy(0, slot, k, 4 * k, dev_yu, 0).start()
            o_copy(0, slot, k, 4 * k + 1, dev_yd, 0).start()

        @pl.loop(0, O_FIRST)
        def _(k):
            o_wait(1, slot, k)
            o_copy(1, slot, k, 16 + 2 * k, dev_yu, 1).start()
            o_copy(1, slot, k, 17 + 2 * k, dev_yd, 1).start()

    project(0, y_dn)
    project(0, y_up)

    @pl.loop(0, Q_FIRST)
    def _(j):
        b_wait(0, y_op, j)

    project(0, y_op)

    @pl.loop(Q_FIRST, Q_CHUNKS)
    def _(j):
        b_wait(1, y, j)

    project(1, y)

    @pl.loop(0, 2)
    def _(n):
        y_ = jnp.where(n == 0, y_dn, y_up)

        @pl.loop(Q_FIRST, Q_CHUNKS)
        def _(j):
            b_wait(1, y_, j)

        project(1, y_)

    @pl.loop(0, Q_CHUNKS)
    def _(j):
        b_wait(1, y_op, j)

    project(1, y_op)

    g_me = group_of(t)

    def rotated(x):
        return x * cos[...] + pltpu.roll(x, 64, 1) * sin[...]

    bias_kv = jnp.where(c == 0, bk[pl.ds(g_me // 2, 1), :], bv[pl.ds(g_me // 2, 1), :])
    raw = acc[:, 512:640] + bias_kv
    kv_own[...] = jnp.where(c == 0, rotated(raw), raw).astype(jnp.bfloat16)
    kv_swap = remote(kv_own, kv_oth, kv_sem.at[0], kv_sem.at[1], dev_kv)
    kv_swap.start()

    for h in range(4):
        cols = slice(h * 128, (h + 1) * 128)
        raw_q = acc[:, cols] + bq[pl.ds(g_me * 4 + h, 1), :]
        qb[:, cols] = rotated(raw_q).astype(jnp.bfloat16)

    kv_swap.wait()
    keys = jnp.where(c == 0, kv_own[...], kv_oth[...])
    values = jnp.where(c == 0, kv_oth[...], kv_own[...])
    kv_own[...] = keys
    kv_oth[...] = values

    def t_ref(src_t, h):
        return att.at[group_of(src_t), pl.ds(pl.multiple_of(h * 256, 256), 256)]

    def t_copy(src_t, h, n, device):
        ref = t_ref(src_t, h)
        return remote(ref, ref, t_send.at[n], t_recv.at[src_t, h], device)

    def t_wait(src_t, h):
        ref = t_ref(src_t, h)
        remote(ref, ref, t_send.at[0], t_recv.at[src_t, h], dev_sib).wait_recv()

    def tid(xh_, z_, c_):
        return xh_ * 8 + z_ * 2 + c_

    def gather_side(copy, wait, chunks, first, side):
        xs = (xh + side) % 2
        own, dn, up = tid(xs, z, c), tid(xs, z_dn, c), tid(xs, z_up, c)
        if side == 1:

            @pl.loop(0, chunks)
            def _(h):
                wait(own, h)

                @pl.when(h < first)
                def _():
                    copy(own, h, 15 * h + 8, dev_zu).start()
                    copy(own, h, 15 * h + 9, dev_zd).start()

                copy(own, h, 15 * h + 10, dev_sib).start()

        @pl.loop(0, chunks)
        def _(h):
            n = 15 * h + 4 + 7 * side
            wait(dn, h)
            wait(up, h)
            along = h < first if side == 1 else h >= 0

            @pl.when(jnp.logical_and(along, h % 2 == 0))
            def _():
                copy(dn, h, n, dev_zu).start()

            @pl.when(jnp.logical_and(along, h % 2 == 1))
            def _():
                copy(up, h, n, dev_zd).start()

            if side == 0:

                @pl.when(h >= first)
                def _():
                    copy(dn, h, 15 * h + 8, dev_xh).start()
                    copy(up, h, 15 * h + 9, dev_xh).start()

            copy(dn, h, n + 1, dev_sib).start()
            copy(up, h, n + 2, dev_sib).start()

    def gather_last(copy, wait, chunks, first, side):
        @pl.loop(0, chunks)
        def _(h):
            op = tid((xh + side) % 2, z_op, c)
            wait(op, h)
            if side == 0:

                @pl.when(h >= first)
                def _():
                    copy(op, h, 15 * h + 11, dev_xh).start()

            copy(op, h, 15 * h + 7 + 7 * side, dev_sib).start()

    def start_own(copy, h):
        copy(t, h, 15 * h, dev_xh).start()
        copy(t, h, 15 * h + 1, dev_zu).start()
        copy(t, h, 15 * h + 2, dev_zd).start()
        copy(t, h, 15 * h + 3, dev_sib).start()

    def wait_sibling(wait, chunks):
        @pl.loop(0, 8)
        def _(n):
            @pl.loop(0, chunks)
            def _(h):
                wait(n * 2 + 1 - c, h)

    length = len_ref[0]

    for n in range(2):
        lo, hi = n * 256, (n + 1) * 256

        @pl.loop(0, 4)
        def _(h):
            cols = pl.ds(pl.multiple_of(h * 128, 128), 128)
            s = lax.dot_general(
                qb[lo:hi, cols], kv_own[0:hi, :], (((1,), (1,)), ((), ())), preferred_element_type=jnp.float32
            ) * HD ** (-0.5)
            r = lax.broadcasted_iota(jnp.int32, (256, hi), 0) + lo
            k = lax.broadcasted_iota(jnp.int32, (256, hi), 1)
            s = jnp.where((k <= r) & (k < length), s, -1e30)
            e = jnp.exp(s - jnp.max(s, axis=1, keepdims=True))
            p = (e / jnp.sum(e, axis=1, keepdims=True)).astype(jnp.bfloat16)
            o = jnp.dot(p, kv_oth[0:hi, :], preferred_element_type=jnp.float32)
            att[g_me, lo:hi, cols] = o.astype(jnp.bfloat16)

        start_own(t_copy, n)

    @pl.when(source)
    def _():
        @pl.loop(O_FIRST, O_CHUNKS)
        def _(k):
            o_copy(0, slot, k, 4 * k + 2, dev_xp, 1).start()

    @pl.when(jnp.logical_not(source))
    def _():
        @pl.loop(0, O_CHUNKS)
        def _(k):
            o_wait(0, s_dn, k)
            o_wait(0, s_up, k)
            o_forward(0, k, 4 * k)

            @pl.when(k >= O_FIRST)
            def _():
                o_copy(0, s_dn, k, 4 * k + 1, dev_xp, 1).start()
                o_copy(0, s_up, k, 4 * k + 2, dev_xp, 1).start()

        @pl.loop(0, O_FIRST)
        def _(k):
            o_wait(1, s_dn, k)
            o_wait(1, s_up, k)
            o_forward(1, k, 4 * k + 1)

    gather_side(t_copy, t_wait, 2, 2, 0)

    @pl.when(source)
    def _():
        @pl.loop(0, O_CHUNKS)
        def _(k):
            o_wait(0, 1 - slot, k)

            @pl.when(k >= O_FIRST)
            def _():
                o_copy(0, 1 - slot, k, 4 * k + 3, dev_xp, 1).start()

    gather_side(t_copy, t_wait, 2, 2, 1)
    gather_last(t_copy, t_wait, 2, 2, 0)

    @pl.when(source)
    def _():
        @pl.loop(O_FIRST, O_CHUNKS)
        def _(k):
            o_wait(1, slot, k)

        @pl.loop(0, O_CHUNKS)
        def _(k):
            o_wait(1, 1 - slot, k)

    @pl.when(jnp.logical_not(source))
    def _():
        @pl.loop(O_FIRST, O_CHUNKS)
        def _(k):
            o_wait(1, s_dn, k)
            o_wait(1, s_up, k)

    def add_group(src_t, first=False):
        g = group_of(src_t)
        part = lax.dot_general(
            att[g],
            wobuf[:, pl.ds(pl.multiple_of(g * 512, 512), 512)],
            (((1,), (1,)), ((), ())),
            preferred_element_type=jnp.float32,
        )
        if first:
            acc2[...] = part
        else:
            acc2[...] += part

    def near(i):
        step = i % 4
        return (xh + i // 4) % 2, (z + ring(step)) % 4

    add_group(t, True)

    @pl.loop(1, 7)
    def _(i):
        xs, zs = near(i)
        add_group(tid(xs, zs, c))

    gather_last(t_copy, t_wait, 2, 2, 1)
    add_group(tid(1 - xh, z_op, c))

    @pl.loop(0, 8)
    def _(i):
        xs, zs = near(i)
        src = tid(xs, zs, 1 - c)
        t_wait(src, 0)
        t_wait(src, 1)
        add_group(src)

    def out_block(src_t, j):
        xh_s, z_s, c_s = src_t // 8, (src_t // 2) % 4, src_t % 2
        side, s = j // 2, j % 2
        xl_b = (xl + side) % 2
        xh_b = (xh_s + side * c_s) % 2
        return (xl_b * 4 + c_s + 2 * s) * 8 + xh_b * 4 + z_s

    def g_ref(src_t, j):
        return out.at[:, pl.ds(pl.multiple_of(out_block(src_t, j) * 128, 128), 128)]

    def g_copy_own(src_t, j, n, device):
        return remote(outb.at[j], g_ref(src_t, j), g_send.at[n], g_recv.at[src_t, j], device)

    def g_copy(src_t, j, n, device):
        ref = g_ref(src_t, j)
        return remote(ref, ref, g_send.at[n], g_recv.at[src_t, j], device)

    def g_wait(src_t, j):
        ref = g_ref(src_t, j)
        remote(ref, ref, g_send.at[0], g_recv.at[src_t, j], dev_sib).wait_recv()

    for j in range(4):
        outb[j] = acc2[:, j * 128 : (j + 1) * 128].astype(jnp.bfloat16)
        pltpu.make_async_copy(outb.at[j], g_ref(t, j), g_loc.at[j]).start()
        start_own(g_copy_own, j)

    gather_side(g_copy, g_wait, 4, G_FIRST, 0)
    gather_last(g_copy, g_wait, 4, G_FIRST, 0)
    gather_side(g_copy, g_wait, 4, G_FIRST, 1)
    gather_last(g_copy, g_wait, 4, G_FIRST, 1)
    wait_sibling(g_wait, 4)

    for j in range(4):
        pltpu.make_async_copy(outb.at[j], g_ref(t, j), g_loc.at[j]).wait()

    def drain(ref, sem):
        remote(ref, ref, sem, sem, dev_sib).wait_send()

    @pl.loop(1, 16)
    def _(i):
        drain(send_a.at[0], a_send.at[(t + i) % 16])

    @pl.when(jnp.logical_not(source))
    def _():
        drain(send_o, sib_sem.at[1])

    @pl.loop(0, 56)
    def _(n):
        drain(wbuf.at[0:128], b_send.at[n])

    @pl.when(source)
    def _():
        @pl.loop(0, O_CHUNKS)
        def _(k):
            for n in range(3):
                drain(wobuf.at[0:32], o_send.at[4 * k + n])

            @pl.when(k >= O_FIRST)
            def _():
                drain(wobuf.at[0:32], o_send.at[4 * k + 3])

            @pl.when(k < O_FIRST)
            def _():
                drain(wobuf.at[0:32], o_send.at[16 + 2 * k])
                drain(wobuf.at[0:32], o_send.at[17 + 2 * k])

    @pl.when(jnp.logical_not(source))
    def _():
        @pl.loop(0, O_CHUNKS)
        def _(k):
            drain(wobuf.at[0:32], o_send.at[4 * k])
            drain(wobuf.at[0:32], o_send.at[4 * k + 1])

            @pl.when(k >= O_FIRST)
            def _():
                drain(wobuf.at[0:32], o_send.at[4 * k + 2])

    @pl.loop(0, 30)
    def _(n):
        drain(att.at[0, 0:256], t_send.at[n])

    @pl.loop(0, 60)
    def _(n):
        drain(outb.at[0], g_send.at[n])


def local(hidden, lengths, norm_gain, w_q, w_k, w_v, w_out, b_q, b_k, b_v):
    positions = np.arange(TOK, dtype=np.float32)
    freqs = np.float32(THETA) ** (-np.arange(0, HD, 2, dtype=np.float32) / np.float32(HD))
    angles = (positions[:, None] * freqs[None, :]).astype(np.float64)
    cosine, sine = np.cos(angles), np.sin(angles)
    cos = np.concatenate((cosine, cosine), axis=1).astype(np.float32)
    sin = np.concatenate((-sine, sine), axis=1).astype(np.float32)
    anywhere = pl.BlockSpec(memory_space=pl.ANY)
    vmem = pl.BlockSpec(memory_space=pltpu.VMEM)
    bf, f32 = jnp.bfloat16, jnp.float32
    dma = pltpu.SemaphoreType.DMA
    result = pl.pallas_call(
        kernel,
        out_shape=jax.ShapeDtypeStruct((TOK, D), bf),
        in_specs=[pl.BlockSpec(memory_space=pltpu.SMEM), anywhere, vmem]
        + [anywhere] * 4
        + [vmem] * 5,
        out_specs=anywhere,
        scratch_shapes=[
            pltpu.VMEM((ROWS, 18432), f32),
            pltpu.VMEM((144, 8, 128), f32),
            pltpu.VMEM((144, 128), f32),
            pltpu.VMEM((144, 128), f32),
            pltpu.VMEM((144, 128), f32),
            pltpu.VMEM((TOK, D), bf),
            pltpu.VMEM((GROUPS, ROWS, WCOLS), bf),
            pltpu.VMEM((D, WCOLS), bf),
            pltpu.VMEM((ROWS, D), bf),
            pltpu.VMEM((512, D), bf),
            pltpu.VMEM((TOK, WCOLS), f32),
            pltpu.VMEM((TOK, GCOLS), bf),
            pltpu.VMEM((TOK, HD), bf),
            pltpu.VMEM((TOK, HD), bf),
            pltpu.VMEM((GROUPS, TOK, GCOLS), bf),
            pltpu.VMEM((TOK, GCOLS), f32),
            pltpu.VMEM((4, TOK, 128), bf),
            dma((5,)),
            dma((2,)),
            dma((16,)),
            dma((16,)),
            dma((56,)),
            dma((2, 4, Q_CHUNKS)),
            dma((3,)),
            dma((20,)),
            dma((2, 2, 4)),
            dma((2,)),
            dma((30,)),
            dma((16, 2)),
            dma((60,)),
            dma((16, 4)),
            dma((4,)),
        ],
        compiler_params=pltpu.CompilerParams(
            collective_id=0, has_side_effects=True, vmem_limit_bytes=62 * 2**20
        ),
    )(
        lengths, hidden[0], norm_gain.reshape(1, D), w_q, w_k, w_v, w_out,
        b_q.reshape(HQ, HD), b_k.reshape(KV, HD), b_v.reshape(KV, HD), cos, sin,
    )
    return result[None]


def solution(mesh):
    rows = P(("dp", "tensor"), None)
    placed = (P("dp", None, None), P("dp"), P(), rows, rows, rows, rows, P(), P(), P())
    return jax.shard_map(
        local, mesh=mesh, in_specs=placed, out_specs=P("dp", None, None), check_vma=False
    )
```

```python
import functools

import jax
import jax.numpy as jnp
import numpy as np
from jax import lax
from jax.experimental import pallas as pl
from jax.experimental.pallas import tpu as pltpu
from jax.sharding import PartitionSpec as P

D = 8192
HQ = 64
KV = 8
HD = 128
TILE = 128
TOK = 512
GROUPS = 16
GCOLS = 512
WCOLS = 640
ROWS = 64
THETA = 1000000.0
NORM_EPS = 1e-06
PEAK_EPS = 1e-06
LEVEL_TOP = 127.0
MESH = pl.DeviceIdType.MESH
QT = 64
KT = 8
Q_CHUNKS = 8
Q_FIRST = 1
O_CHUNKS = 4
O_FIRST = 2
O_EARLY = 2
O_MID = 3
G_FIRST = 2


def kernel(
    len_ref, hid_hbm, gain_hbm, wq, wk, wv, wo, bq_hbm, bk_hbm, bv_hbm, cos_hbm, sin_hbm, out,
    gain, bq, bk, bv, cos, sin, wf, pm, pk_own, pk_oth, sc, hid, send_a, wbuf, send_o, wobuf, acc, qb, kv_own, kv_oth, att, acc2, outb,
    ld_sem, pk_sem, a_send, a_recv, b_send, b_recv, sib_sem, o_send, o_recv, kv_sem, t_send, t_recv, g_send, g_recv, g_loc,
):
    dp = lax.axis_index("dp")
    t = lax.axis_index("tensor")
    xl, y = dp // 4, dp % 4
    xh, z, c = t // 8, (t // 2) % 4, t % 2

    def dev(xl_, y_, xh_, z_, c_):
        return (xl_ * 4 + y_, xh_ * 8 + z_ * 2 + c_)

    y_up, y_dn, y_op = (y + 1) % 4, (y + 3) % 4, (y + 2) % 4
    z_up, z_dn, z_op = (z + 1) % 4, (z + 3) % 4, (z + 2) % 4
    dev_yu, dev_yd = dev(xl, y_up, xh, z, c), dev(xl, y_dn, xh, z, c)
    dev_xp = dev(1 - xl, y, (xh + c) % 2, z, c)
    dev_zu, dev_zd = dev(xl, y, xh, z_up, c), dev(xl, y, xh, z_dn, c)
    dev_xh = dev(xl, y, 1 - xh, z, c)
    dev_sib = dev(xl, y, xh, z, 1 - c)
    dev_kv = dev(xl, y, (xh + xl) % 2, z, 1 - c)

    def group_of(t_):
        return ((t_ // 8 + (t_ % 2) * xl) % 2) * 8 + t_ % 8

    def remote(src, dst, ss, rs, device):
        return pltpu.make_async_remote_copy(
            src_ref=src, dst_ref=dst, send_sem=ss, recv_sem=rs, device_id=device, device_id_type=MESH
        )

    loads = (
        pltpu.make_async_copy(wq, wf.at[:, 0:8192], ld_sem.at[0]),
        pltpu.make_async_copy(wk, wf.at[:, 8192:9216], ld_sem.at[1]),
        pltpu.make_async_copy(wv, wf.at[:, 9216:10240], ld_sem.at[2]),
        pltpu.make_async_copy(wo, wf.at[:, 10240:18432], ld_sem.at[3]),
        pltpu.make_async_copy(hid_hbm, hid, ld_sem.at[4]),
        pltpu.make_async_copy(gain_hbm, gain, ld_sem.at[5]),
        pltpu.make_async_copy(bq_hbm, bq, ld_sem.at[6]),
        pltpu.make_async_copy(bk_hbm, bk, ld_sem.at[7]),
        pltpu.make_async_copy(bv_hbm, bv, ld_sem.at[8]),
        pltpu.make_async_copy(cos_hbm, cos, ld_sem.at[9]),
        pltpu.make_async_copy(sin_hbm, sin, ld_sem.at[10]),
    )
    for cp in loads:
        cp.start()

    barrier = pltpu.get_barrier_semaphore()

    @pl.loop(1, 16)
    def _(i):
        pl.semaphore_signal(barrier, inc=1, device_id=(dp, (t + i) % 16), device_id_type=MESH)

    for peer in (dev_yu, dev_yd, dev_xp):
        pl.semaphore_signal(barrier, inc=1, device_id=peer, device_id_type=MESH)

    for cp in loads[:4]:
        cp.wait()

    @pl.loop(0, 144, unroll=4)
    def _(j):
        tile = jnp.abs(wf[:, pl.ds(pl.multiple_of(j * 128, 128), 128)])
        pm[j] = jnp.max(tile.reshape(8, 8, 128), axis=0)

    peaks = jnp.max(jnp.max(pm[...], axis=1), axis=1, keepdims=True)
    pk_own[...] = jnp.broadcast_to(peaks, (144, 128))

    pl.semaphore_wait(barrier, 18)
    swap = remote(pk_own, pk_oth, pk_sem.at[0], pk_sem.at[1], dev_sib)
    swap.start()
    swap.wait()
    full = jnp.maximum(pk_own[...], pk_oth[...])
    sc[...] = ((full + PEAK_EPS) / LEVEL_TOP).astype(jnp.bfloat16).astype(jnp.float32)

    def quantized(j):
        tile = wf[:, pl.ds(pl.multiple_of(j * 128, 128), 128)]
        s = sc[pl.ds(j, 1), :]
        return (jnp.floor(tile / s + 0.5) * s).astype(jnp.bfloat16)

    my_rows = pl.ds(pl.multiple_of(dp * 1024 + t * 64, 64), 64)

    hx = (xh + c * xl) % 2

    def ring(step):
        return jnp.where(step == 1, 3, jnp.where(step == 2, 1, jnp.where(step == 3, 2, 0)))

    @pl.loop(0, 16)
    def _(i):
        to_c = i % 2
        to = ((xh + i // 8 + to_c * xl) % 2) * 8 + ((z + 4 - ring((i // 2) % 4)) % 4) * 2 + to_c
        g = group_of(to)
        for n in range(4):
            send_a[g, :, n * 128 : (n + 1) * 128] = quantized(g * 4 + n)
        send_a[g, :, 512:640] = quantized(QT + KT * to_c + g // 2)

        @pl.when(to == t)
        def _():
            pltpu.make_async_copy(send_a.at[g], wbuf.at[my_rows], a_recv.at[t]).start()

        @pl.when(to != t)
        def _():
            remote(send_a.at[g], wbuf.at[my_rows], a_send.at[to], a_recv.at[t], (dp, to)).start()

    source = y % 2 == c
    slot = y // 2

    @pl.loop(0, 64)
    def _(j):
        send_o[:, pl.ds(pl.multiple_of(j * 128, 128), 128)] = quantized(QT + 2 * KT + j)

    half_rows = pl.ds(pl.multiple_of((y // 2) * 128 + c * 64, 64), 64)

    @pl.when(source)
    def _():
        pltpu.make_async_copy(send_o, wobuf.at[half_rows], sib_sem.at[0]).start()

    @pl.when(jnp.logical_not(source))
    def _():
        remote(send_o, wobuf.at[half_rows], sib_sem.at[1], sib_sem.at[2], dev_sib).start()

    for cp in loads[4:]:
        cp.wait()

    @pl.loop(0, 32)
    def _(i):
        rows = pl.ds(pl.multiple_of(i * 16, 16), 16)
        wide = hid[rows, :].astype(jnp.float32)
        ms = jnp.mean(wide * wide, axis=1, keepdims=True)
        hid[rows, :] = (wide * lax.rsqrt(ms + NORM_EPS) * gain[...]).astype(jnp.bfloat16)

    def o_rows(side, s, k):
        return pl.ds(pl.multiple_of(side * 256 + s * 128 + k * 32, 32), 32)

    def o_copy(side, s, k, n, device, to_side):
        return remote(
            wobuf.at[o_rows(side, s, k)], wobuf.at[o_rows(to_side, s, k)], o_send.at[n],
            o_recv.at[to_side, s, k], device,
        )

    def o_wait(side, s, k):
        ref = wobuf.at[o_rows(side, s, k)]
        remote(ref, ref, o_send.at[0], o_recv.at[side, s, k], dev_xp).wait_recv()

    s_dn, s_up = y_dn // 2, y_up // 2

    def o_forward(side, k, n):
        @pl.when(k % 2 == 0)
        def _():
            o_copy(side, s_dn, k, n, dev_yu, side).start()

        @pl.when(k % 2 == 1)
        def _():
            o_copy(side, s_up, k, n, dev_yd, side).start()

    def b_chip(j):
        return ((hx + j // 4) % 2) * 4 + (z + ring(j % 4)) % 4

    def b_rows(side, y_, j):
        return pl.ds(pl.multiple_of((((xl + side) % 2) * 4 + y_) * 1024 + b_chip(j) * 128, 128), 128)

    def b_copy(side, y_, j, n, device, to_side):
        ref = wbuf.at[b_rows(side, y_, j)]
        return remote(ref, ref, b_send.at[n], b_recv.at[to_side, y_, j], device)

    def b_wait(side, y_, j):
        ref = wbuf.at[b_rows(side, y_, j)]
        remote(ref, ref, b_send.at[0], b_recv.at[side, y_, j], dev_xp).wait_recv()

    def b_forward(side, j, n):
        @pl.when(j % 2 == 0)
        def _():
            b_copy(side, y_dn, j, n, dev_yu, side).start()

        @pl.when(j % 2 == 1)
        def _():
            b_copy(side, y_up, j, n, dev_yd, side).start()

    def project(side, y_, first=False):
        base = (((xl + side) % 2) * 4 + y_) * 1024
        for n in range(2):
            cols = pl.ds(pl.multiple_of(base + n * 512, 512), 512)
            part = jnp.dot(hid[:, cols], wbuf[cols, :], preferred_element_type=jnp.float32)
            if first and n == 0:
                acc[...] = part
            else:
                acc[...] += part

    @pl.when(source)
    def _():
        pltpu.make_async_copy(send_o, wobuf.at[half_rows], sib_sem.at[0]).wait()
        remote(send_o, wobuf.at[half_rows], sib_sem.at[1], sib_sem.at[2], dev_sib).wait_recv()

        @pl.loop(0, O_EARLY)
        def _(k):
            o_copy(0, slot, k, 4 * k, dev_yu, 0).start()
            o_copy(0, slot, k, 4 * k + 1, dev_yd, 0).start()

    @pl.loop(0, Q_CHUNKS)
    def _(j):
        @pl.loop(0, 2)
        def _(n):
            src_t = b_chip(j) * 2 + n
            rows = pl.ds(pl.multiple_of(dp * 1024 + src_t * 64, 64), 64)
            ref = wbuf.at[rows]
            remote(ref, ref, a_send.at[0], a_recv.at[src_t], dev_xp).wait_recv()

        b_copy(0, y, j, 3 * j, dev_xp, 1).start()
        b_copy(0, y, j, 3 * j + 1, dev_yu, 0).start()
        b_copy(0, y, j, 3 * j + 2, dev_yd, 0).start()

    @pl.when(source)
    def _():
        @pl.loop(0, O_FIRST)
        def _(k):
            o_copy(0, slot, k, 4 * k + 2, dev_xp, 1).start()

    @pl.loop(0, Q_FIRST)
    def _(j):
        n = 24 + 4 * j
        b_wait(1, y, j)
        b_copy(1, y, j, n, dev_yu, 1).start()
        b_copy(1, y, j, n + 1, dev_yd, 1).start()
        b_wait(0, y_dn, j)
        b_wait(0, y_up, j)
        b_forward(0, j, n + 2)

    @pl.loop(Q_FIRST, Q_CHUNKS)
    def _(j):
        n = 24 + 4 * j
        b_wait(0, y_dn, j)
        b_copy(0, y_dn, j, n, dev_xp, 1).start()
        b_wait(0, y_up, j)
        b_copy(0, y_up, j, n + 1, dev_xp, 1).start()
        b_forward(0, j, n + 2)

    @pl.loop(0, Q_FIRST)
    def _(j):
        b_wait(1, y_dn, j)
        b_wait(1, y_up, j)
        b_forward(1, j, 24 + 4 * j + 3)

    project(0, y, first=True)

    @pl.loop(Q_FIRST, Q_CHUNKS)
    def _(j):
        b_wait(0, y_op, j)
        b_copy(0, y_op, j, 24 + 4 * j + 3, dev_xp, 1).start()

    @pl.when(source)
    def _():
        @pl.loop(O_EARLY, O_CHUNKS)
        def _(k):
            o_copy(0, slot, k, 4 * k, dev_yu, 0).start()
            o_copy(0, slot, k, 4 * k + 1, dev_yd, 0).start()

        @pl.loop(0, O_FIRST)
        def _(k):
            o_wait(1, slot, k)
            o_copy(1, slot, k, 16 + 2 * k, dev_yu, 1).start()
            o_copy(1, slot, k, 17 + 2 * k, dev_yd, 1).start()

    def o_pass(k):
        o_wait(0, s_dn, k)
        o_wait(0, s_up, k)

        @pl.when(k >= O_FIRST)
        def _():
            o_copy(0, s_dn, k, 4 * k + 1, dev_xp, 1).start()
            o_copy(0, s_up, k, 4 * k + 2, dev_xp, 1).start()

        o_forward(0, k, 4 * k)

    @pl.when(jnp.logical_not(source))
    def _():
        @pl.loop(0, O_EARLY)
        def _(k):
            o_pass(k)

    project(0, y_dn)
    project(0, y_up)

    @pl.loop(0, Q_FIRST)
    def _(j):
        b_wait(0, y_op, j)

    project(0, y_op)

    @pl.loop(Q_FIRST, Q_CHUNKS)
    def _(j):
        b_wait(1, y, j)

    project(1, y)

    @pl.loop(0, 2)
    def _(n):
        y_ = jnp.where(n == 0, y_dn, y_up)

        @pl.loop(Q_FIRST, Q_CHUNKS)
        def _(j):
            b_wait(1, y_, j)

        project(1, y_)

    @pl.loop(0, Q_CHUNKS)
    def _(j):
        b_wait(1, y_op, j)

    project(1, y_op)

    g_me = group_of(t)

    def rotated(x):
        return x * cos[...] + pltpu.roll(x, 64, 1) * sin[...]

    bias_kv = jnp.where(c == 0, bk[pl.ds(g_me // 2, 1), :], bv[pl.ds(g_me // 2, 1), :])
    raw = acc[:, 512:640] + bias_kv
    kv_own[...] = jnp.where(c == 0, rotated(raw), raw).astype(jnp.bfloat16)
    kv_swap = remote(kv_own, kv_oth, kv_sem.at[0], kv_sem.at[1], dev_kv)
    kv_swap.start()

    @pl.when(source)
    def _():
        @pl.loop(O_FIRST, O_CHUNKS)
        def _(k):
            o_copy(0, slot, k, 4 * k + 2, dev_xp, 1).start()

    @pl.when(jnp.logical_not(source))
    def _():
        @pl.loop(O_EARLY, O_MID)
        def _(k):
            o_pass(k)

    for h in range(4):
        cols = slice(h * 128, (h + 1) * 128)
        raw_q = acc[:, cols] + bq[pl.ds(g_me * 4 + h, 1), :]
        qb[:, cols] = rotated(raw_q).astype(jnp.bfloat16)

    kv_swap.wait()
    keys = jnp.where(c == 0, kv_own[...], kv_oth[...])
    values = jnp.where(c == 0, kv_oth[...], kv_own[...])
    kv_own[...] = keys
    kv_oth[...] = values

    def t_ref(src_t, h):
        return att.at[group_of(src_t), pl.ds(pl.multiple_of(h * 256, 256), 256)]

    def t_copy(src_t, h, n, device):
        ref = t_ref(src_t, h)
        return remote(ref, ref, t_send.at[n], t_recv.at[src_t, h], device)

    def t_wait(src_t, h):
        ref = t_ref(src_t, h)
        remote(ref, ref, t_send.at[0], t_recv.at[src_t, h], dev_sib).wait_recv()

    def tid(xh_, z_, c_):
        return xh_ * 8 + z_ * 2 + c_

    def gather_cross(copy, wait, chunks, first):
        own = tid(1 - xh, z, c)

        @pl.loop(0, chunks)
        def _(h):
            wait(own, h)

            @pl.when(h < first)
            def _():
                copy(own, h, 15 * h + 8, dev_zu).start()
                copy(own, h, 15 * h + 9, dev_zd).start()

            copy(own, h, 15 * h + 10, dev_sib).start()

    def gather_side(copy, wait, chunks, first, side):
        xs = (xh + side) % 2
        dn, up = tid(xs, z_dn, c), tid(xs, z_up, c)
        @pl.loop(0, chunks)
        def _(h):
            n = 15 * h + 4 + 7 * side
            wait(dn, h)
            wait(up, h)
            along = h < first if side == 1 else h >= 0

            @pl.when(jnp.logical_and(along, h % 2 == 0))
            def _():
                copy(dn, h, n, dev_zu).start()

            @pl.when(jnp.logical_and(along, h % 2 == 1))
            def _():
                copy(up, h, n, dev_zd).start()

            if side == 0:

                @pl.when(h >= first)
                def _():
                    copy(dn, h, 15 * h + 8, dev_xh).start()
                    copy(up, h, 15 * h + 9, dev_xh).start()

            copy(dn, h, n + 1, dev_sib).start()
            copy(up, h, n + 2, dev_sib).start()

    def gather_last(copy, wait, chunks, first, side):
        @pl.loop(0, chunks)
        def _(h):
            op = tid((xh + side) % 2, z_op, c)
            wait(op, h)
            if side == 0:

                @pl.when(h >= first)
                def _():
                    copy(op, h, 15 * h + 11, dev_xh).start()

            copy(op, h, 15 * h + 7 + 7 * side, dev_sib).start()

    def start_own(copy, h):
        copy(t, h, 15 * h, dev_xh).start()
        copy(t, h, 15 * h + 1, dev_zu).start()
        copy(t, h, 15 * h + 2, dev_zd).start()
        copy(t, h, 15 * h + 3, dev_sib).start()

    def wait_sibling(wait, chunks):
        @pl.loop(0, 8)
        def _(n):
            @pl.loop(0, chunks)
            def _(h):
                wait(n * 2 + 1 - c, h)

    length = len_ref[0]

    for n in range(2):
        lo, hi = n * 256, (n + 1) * 256

        @pl.loop(0, 4)
        def _(h):
            cols = pl.ds(pl.multiple_of(h * 128, 128), 128)
            s = lax.dot_general(
                qb[lo:hi, cols], kv_own[0:hi, :], (((1,), (1,)), ((), ())), preferred_element_type=jnp.float32
            ) * HD ** (-0.5)
            r = lax.broadcasted_iota(jnp.int32, (256, hi), 0) + lo
            k = lax.broadcasted_iota(jnp.int32, (256, hi), 1)
            s = jnp.where((k <= r) & (k < length), s, -1e30)
            e = jnp.exp(s - jnp.max(s, axis=1, keepdims=True))
            p = (e / jnp.sum(e, axis=1, keepdims=True)).astype(jnp.bfloat16)
            o = jnp.dot(p, kv_oth[0:hi, :], preferred_element_type=jnp.float32)
            att[g_me, lo:hi, cols] = o.astype(jnp.bfloat16)

        start_own(t_copy, n)

    @pl.when(jnp.logical_not(source))
    def _():
        @pl.loop(O_MID, O_CHUNKS)
        def _(k):
            o_wait(0, s_dn, k)
            o_wait(0, s_up, k)
            o_forward(0, k, 4 * k)

        @pl.loop(0, O_FIRST)
        def _(k):
            o_wait(1, s_dn, k)
            o_wait(1, s_up, k)
            o_forward(1, k, 4 * k + 1)

    gather_side(t_copy, t_wait, 2, 2, 0)
    gather_cross(t_copy, t_wait, 2, 2)

    @pl.when(source)
    def _():
        @pl.loop(0, O_CHUNKS)
        def _(k):
            o_wait(0, 1 - slot, k)

            @pl.when(k >= O_FIRST)
            def _():
                o_copy(0, 1 - slot, k, 4 * k + 3, dev_xp, 1).start()

    @pl.when(jnp.logical_not(source))
    def _():
        @pl.loop(O_MID, O_CHUNKS)
        def _(k):
            o_copy(0, s_dn, k, 4 * k + 1, dev_xp, 1).start()
            o_copy(0, s_up, k, 4 * k + 2, dev_xp, 1).start()

    gather_side(t_copy, t_wait, 2, 2, 1)
    gather_last(t_copy, t_wait, 2, 2, 0)

    @pl.when(source)
    def _():
        @pl.loop(O_FIRST, O_CHUNKS)
        def _(k):
            o_wait(1, slot, k)

        @pl.loop(0, O_CHUNKS)
        def _(k):
            o_wait(1, 1 - slot, k)

    @pl.when(jnp.logical_not(source))
    def _():
        @pl.loop(O_FIRST, O_CHUNKS)
        def _(k):
            o_wait(1, s_dn, k)
            o_wait(1, s_up, k)

    def add_group(src_t, first=False):
        g = group_of(src_t)
        part = lax.dot_general(
            att[g],
            wobuf[:, pl.ds(pl.multiple_of(g * 512, 512), 512)],
            (((1,), (1,)), ((), ())),
            preferred_element_type=jnp.float32,
        )
        if first:
            acc2[...] = part
        else:
            acc2[...] += part

    def near(i):
        step = i % 4
        return (xh + i // 4) % 2, (z + ring(step)) % 4

    add_group(t, True)

    @pl.loop(1, 7)
    def _(i):
        xs, zs = near(i)
        add_group(tid(xs, zs, c))

    gather_last(t_copy, t_wait, 2, 2, 1)
    add_group(tid(1 - xh, z_op, c))

    @pl.loop(0, 8)
    def _(i):
        xs, zs = near(i)
        src = tid(xs, zs, 1 - c)
        t_wait(src, 0)
        t_wait(src, 1)
        add_group(src)

    def out_block(src_t, j):
        xh_s, z_s, c_s = src_t // 8, (src_t // 2) % 4, src_t % 2
        side, s = j // 2, j % 2
        xl_b = (xl + side) % 2
        xh_b = (xh_s + side * c_s) % 2
        return (xl_b * 4 + c_s + 2 * s) * 8 + xh_b * 4 + z_s

    def g_ref(src_t, j):
        return out.at[:, pl.ds(pl.multiple_of(out_block(src_t, j) * 128, 128), 128)]

    def g_copy_own(src_t, j, n, device):
        return remote(outb.at[j], g_ref(src_t, j), g_send.at[n], g_recv.at[src_t, j], device)

    def g_copy(src_t, j, n, device):
        ref = g_ref(src_t, j)
        return remote(ref, ref, g_send.at[n], g_recv.at[src_t, j], device)

    def g_wait(src_t, j):
        ref = g_ref(src_t, j)
        remote(ref, ref, g_send.at[0], g_recv.at[src_t, j], dev_sib).wait_recv()

    for j in range(4):
        outb[j] = acc2[:, j * 128 : (j + 1) * 128].astype(jnp.bfloat16)
        pltpu.make_async_copy(outb.at[j], g_ref(t, j), g_loc.at[j]).start()
        start_own(g_copy_own, j)

    gather_side(g_copy, g_wait, 4, G_FIRST, 0)
    gather_last(g_copy, g_wait, 4, G_FIRST, 0)
    gather_cross(g_copy, g_wait, 4, G_FIRST)
    gather_side(g_copy, g_wait, 4, G_FIRST, 1)
    gather_last(g_copy, g_wait, 4, G_FIRST, 1)
    wait_sibling(g_wait, 4)

    for j in range(4):
        pltpu.make_async_copy(outb.at[j], g_ref(t, j), g_loc.at[j]).wait()

    def drain(ref, sem):
        remote(ref, ref, sem, sem, dev_sib).wait_send()

    @pl.loop(1, 16)
    def _(i):
        drain(send_a.at[0], a_send.at[(t + i) % 16])

    @pl.when(jnp.logical_not(source))
    def _():
        drain(send_o, sib_sem.at[1])

    @pl.loop(0, 56)
    def _(n):
        drain(wbuf.at[0:128], b_send.at[n])

    @pl.when(source)
    def _():
        @pl.loop(0, O_CHUNKS)
        def _(k):
            for n in range(3):
                drain(wobuf.at[0:32], o_send.at[4 * k + n])

            @pl.when(k >= O_FIRST)
            def _():
                drain(wobuf.at[0:32], o_send.at[4 * k + 3])

            @pl.when(k < O_FIRST)
            def _():
                drain(wobuf.at[0:32], o_send.at[16 + 2 * k])
                drain(wobuf.at[0:32], o_send.at[17 + 2 * k])

    @pl.when(jnp.logical_not(source))
    def _():
        @pl.loop(0, O_CHUNKS)
        def _(k):
            drain(wobuf.at[0:32], o_send.at[4 * k])
            drain(wobuf.at[0:32], o_send.at[4 * k + 1])

            @pl.when(k >= O_FIRST)
            def _():
                drain(wobuf.at[0:32], o_send.at[4 * k + 2])

    @pl.loop(0, 30)
    def _(n):
        drain(att.at[0, 0:256], t_send.at[n])

    @pl.loop(0, 60)
    def _(n):
        drain(outb.at[0], g_send.at[n])


def local(hidden, lengths, norm_gain, w_q, w_k, w_v, w_out, b_q, b_k, b_v):
    positions = np.arange(TOK, dtype=np.float32)
    freqs = np.float32(THETA) ** (-np.arange(0, HD, 2, dtype=np.float32) / np.float32(HD))
    angles = (positions[:, None] * freqs[None, :]).astype(np.float64)
    cosine, sine = np.cos(angles), np.sin(angles)
    cos = np.concatenate((cosine, cosine), axis=1).astype(np.float32)
    sin = np.concatenate((-sine, sine), axis=1).astype(np.float32)
    anywhere = pl.BlockSpec(memory_space=pl.ANY)
    hbm = pl.BlockSpec(memory_space=pltpu.HBM)
    bf, f32 = jnp.bfloat16, jnp.float32
    dma = pltpu.SemaphoreType.DMA
    result = pl.pallas_call(
        kernel,
        out_shape=jax.ShapeDtypeStruct((TOK, D), bf),
        in_specs=[pl.BlockSpec(memory_space=pltpu.SMEM)] + [hbm] * 11,
        out_specs=anywhere,
        scratch_shapes=[
            pltpu.VMEM((1, D), f32),
            pltpu.VMEM((HQ, HD), f32),
            pltpu.VMEM((KV, HD), f32),
            pltpu.VMEM((KV, HD), f32),
            pltpu.VMEM((TOK, HD), f32),
            pltpu.VMEM((TOK, HD), f32),
            pltpu.VMEM((ROWS, 18432), f32),
            pltpu.VMEM((144, 8, 128), f32),
            pltpu.VMEM((144, 128), f32),
            pltpu.VMEM((144, 128), f32),
            pltpu.VMEM((144, 128), f32),
            pltpu.VMEM((TOK, D), bf),
            pltpu.VMEM((GROUPS, ROWS, WCOLS), bf),
            pltpu.VMEM((D, WCOLS), bf),
            pltpu.VMEM((ROWS, D), bf),
            pltpu.VMEM((512, D), bf),
            pltpu.VMEM((TOK, WCOLS), f32),
            pltpu.VMEM((TOK, GCOLS), bf),
            pltpu.VMEM((TOK, HD), bf),
            pltpu.VMEM((TOK, HD), bf),
            pltpu.VMEM((GROUPS, TOK, GCOLS), bf),
            pltpu.VMEM((TOK, GCOLS), f32),
            pltpu.VMEM((4, TOK, 128), bf),
            dma((11,)),
            dma((2,)),
            dma((16,)),
            dma((16,)),
            dma((56,)),
            dma((2, 4, Q_CHUNKS)),
            dma((3,)),
            dma((20,)),
            dma((2, 2, 4)),
            dma((2,)),
            dma((30,)),
            dma((16, 2)),
            dma((60,)),
            dma((16, 4)),
            dma((4,)),
        ],
        compiler_params=pltpu.CompilerParams(
            collective_id=0, has_side_effects=True, vmem_limit_bytes=62 * 2**20
        ),
    )(
        lengths, hidden[0], norm_gain.reshape(1, D), w_q, w_k, w_v, w_out,
        b_q.reshape(HQ, HD), b_k.reshape(KV, HD), b_v.reshape(KV, HD), cos, sin,
    )
    return result[None]


def solution(mesh):
    rows = P(("dp", "tensor"), None)
    placed = (P("dp", None, None), P("dp"), P(), rows, rows, rows, rows, P(), P(), P())
    return jax.shard_map(
        local, mesh=mesh, in_specs=placed, out_specs=P("dp", None, None), check_vma=False
    )
```

```python
import functools

import jax
import jax.numpy as jnp
import numpy as np
from jax import lax
from jax.experimental import pallas as pl
from jax.experimental.pallas import tpu as pltpu
from jax.sharding import PartitionSpec as P

D = 8192
HQ = 64
KV = 8
HD = 128
TILE = 128
TOK = 512
GROUPS = 16
GCOLS = 512
WCOLS = 640
ROWS = 64
THETA = 1000000.0
NORM_EPS = 1e-06
PEAK_EPS = 1e-06
LEVEL_TOP = 127.0
MESH = pl.DeviceIdType.MESH
QT = 64
KT = 8
Q_CHUNKS = 8
Q_FIRST = 1
O_CHUNKS = 8
O_ROWS = 16
O_FIRST = 4
O_EARLY = 0
O_MID = 6
T_CHUNKS = 4
T_ROWS = 128
G_CHUNKS = 8
G_FIRST = 4


def kernel(
    len_ref, hid_hbm, gain_hbm, wq, wk, wv, wo, bq_hbm, bk_hbm, bv_hbm, cos_hbm, sin_hbm, out,
    gain, bq, bk, bv, cos, sin, wf, pm, pk_own, pk_oth, sc, hid, send_a, wbuf, send_o, wobuf, acc, qb, kv_own, kv_oth, att, acc2, outb,
    ld_sem, pk_sem, a_send, a_recv, b_send, b_recv, sib_sem, o_send, o_recv, kv_sem, t_send, t_recv, g_send, g_recv, g_loc,
):
    dp = lax.axis_index("dp")
    t = lax.axis_index("tensor")
    xl, y = dp // 4, dp % 4
    xh, z, c = t // 8, (t // 2) % 4, t % 2

    def dev(xl_, y_, xh_, z_, c_):
        return (xl_ * 4 + y_, xh_ * 8 + z_ * 2 + c_)

    y_up, y_dn, y_op = (y + 1) % 4, (y + 3) % 4, (y + 2) % 4
    z_up, z_dn, z_op = (z + 1) % 4, (z + 3) % 4, (z + 2) % 4
    dev_yu, dev_yd = dev(xl, y_up, xh, z, c), dev(xl, y_dn, xh, z, c)
    dev_xp = dev(1 - xl, y, (xh + c) % 2, z, c)
    dev_zu, dev_zd = dev(xl, y, xh, z_up, c), dev(xl, y, xh, z_dn, c)
    dev_xh = dev(xl, y, 1 - xh, z, c)
    dev_sib = dev(xl, y, xh, z, 1 - c)
    dev_kv = dev(xl, y, (xh + xl) % 2, z, 1 - c)

    def group_of(t_):
        return ((t_ // 8 + (t_ % 2) * xl) % 2) * 8 + t_ % 8

    def remote(src, dst, ss, rs, device):
        return pltpu.make_async_remote_copy(
            src_ref=src, dst_ref=dst, send_sem=ss, recv_sem=rs, device_id=device, device_id_type=MESH
        )

    loads = (
        pltpu.make_async_copy(wq, wf.at[:, 0:8192], ld_sem.at[0]),
        pltpu.make_async_copy(wk, wf.at[:, 8192:9216], ld_sem.at[1]),
        pltpu.make_async_copy(wv, wf.at[:, 9216:10240], ld_sem.at[2]),
        pltpu.make_async_copy(wo, wf.at[:, 10240:18432], ld_sem.at[3]),
        pltpu.make_async_copy(hid_hbm, hid, ld_sem.at[4]),
        pltpu.make_async_copy(gain_hbm, gain, ld_sem.at[5]),
        pltpu.make_async_copy(bq_hbm, bq, ld_sem.at[6]),
        pltpu.make_async_copy(bk_hbm, bk, ld_sem.at[7]),
        pltpu.make_async_copy(bv_hbm, bv, ld_sem.at[8]),
        pltpu.make_async_copy(cos_hbm, cos, ld_sem.at[9]),
        pltpu.make_async_copy(sin_hbm, sin, ld_sem.at[10]),
    )
    for cp in loads:
        cp.start()

    barrier = pltpu.get_barrier_semaphore()

    @pl.loop(1, 16)
    def _(i):
        pl.semaphore_signal(barrier, inc=1, device_id=(dp, (t + i) % 16), device_id_type=MESH)

    for peer in (dev_yu, dev_yd, dev_xp):
        pl.semaphore_signal(barrier, inc=1, device_id=peer, device_id_type=MESH)

    for cp in loads[:4]:
        cp.wait()

    @pl.loop(0, 144, unroll=4)
    def _(j):
        tile = jnp.abs(wf[:, pl.ds(pl.multiple_of(j * 128, 128), 128)])
        pm[j] = jnp.max(tile.reshape(8, 8, 128), axis=0)

    peaks = jnp.max(jnp.max(pm[...], axis=1), axis=1, keepdims=True)
    pk_own[...] = jnp.broadcast_to(peaks, (144, 128))

    pl.semaphore_wait(barrier, 18)
    swap = remote(pk_own, pk_oth, pk_sem.at[0], pk_sem.at[1], dev_sib)
    swap.start()
    swap.wait()
    full = jnp.maximum(pk_own[...], pk_oth[...])
    sc[...] = ((full + PEAK_EPS) / LEVEL_TOP).astype(jnp.bfloat16).astype(jnp.float32)

    def quantized(j):
        tile = wf[:, pl.ds(pl.multiple_of(j * 128, 128), 128)]
        s = sc[pl.ds(j, 1), :]
        return (jnp.floor(tile / s + 0.5) * s).astype(jnp.bfloat16)

    my_rows = pl.ds(pl.multiple_of(dp * 1024 + t * 64, 64), 64)

    hx = (xh + c * xl) % 2

    def ring(step):
        return jnp.where(step == 1, 3, jnp.where(step == 2, 1, jnp.where(step == 3, 2, 0)))

    @pl.loop(0, 16)
    def _(i):
        to_c = i % 2
        to = ((xh + i // 8 + to_c * xl) % 2) * 8 + ((z + 4 - ring((i // 2) % 4)) % 4) * 2 + to_c
        g = group_of(to)
        for n in range(4):
            send_a[g, :, n * 128 : (n + 1) * 128] = quantized(g * 4 + n)
        send_a[g, :, 512:640] = quantized(QT + KT * to_c + g // 2)

        @pl.when(to == t)
        def _():
            pltpu.make_async_copy(send_a.at[g], wbuf.at[my_rows], a_recv.at[t]).start()

        @pl.when(to != t)
        def _():
            remote(send_a.at[g], wbuf.at[my_rows], a_send.at[to], a_recv.at[t], (dp, to)).start()

    source = y % 2 == c
    slot = y // 2

    @pl.loop(0, 64)
    def _(j):
        send_o[:, pl.ds(pl.multiple_of(j * 128, 128), 128)] = quantized(QT + 2 * KT + j)

    half_rows = pl.ds(pl.multiple_of((y // 2) * 128 + c * 64, 64), 64)

    @pl.when(source)
    def _():
        pltpu.make_async_copy(send_o, wobuf.at[half_rows], sib_sem.at[0]).start()

    @pl.when(jnp.logical_not(source))
    def _():
        remote(send_o, wobuf.at[half_rows], sib_sem.at[1], sib_sem.at[2], dev_sib).start()

    for cp in loads[4:]:
        cp.wait()

    @pl.loop(0, 32)
    def _(i):
        rows = pl.ds(pl.multiple_of(i * 16, 16), 16)
        wide = hid[rows, :].astype(jnp.float32)
        ms = jnp.mean(wide * wide, axis=1, keepdims=True)
        hid[rows, :] = (wide * lax.rsqrt(ms + NORM_EPS) * gain[...]).astype(jnp.bfloat16)

    def o_rows(side, s, k):
        return pl.ds(pl.multiple_of(side * 256 + s * 128 + k * O_ROWS, O_ROWS), O_ROWS)

    def o_copy(side, s, k, n, device, to_side):
        return remote(
            wobuf.at[o_rows(side, s, k)], wobuf.at[o_rows(to_side, s, k)], o_send.at[n],
            o_recv.at[to_side, s, k], device,
        )

    def o_wait(side, s, k):
        ref = wobuf.at[o_rows(side, s, k)]
        remote(ref, ref, o_send.at[0], o_recv.at[side, s, k], dev_xp).wait_recv()

    s_dn, s_up = y_dn // 2, y_up // 2

    def o_forward(side, k, n):
        @pl.when(k % 2 == 0)
        def _():
            o_copy(side, s_dn, k, n, dev_yu, side).start()

        @pl.when(k % 2 == 1)
        def _():
            o_copy(side, s_up, k, n, dev_yd, side).start()

    def b_chip(j):
        return ((hx + j // 4) % 2) * 4 + (z + ring(j % 4)) % 4

    def b_rows(side, y_, j):
        return pl.ds(pl.multiple_of((((xl + side) % 2) * 4 + y_) * 1024 + b_chip(j) * 128, 128), 128)

    def b_copy(side, y_, j, n, device, to_side):
        ref = wbuf.at[b_rows(side, y_, j)]
        return remote(ref, ref, b_send.at[n], b_recv.at[to_side, y_, j], device)

    def b_wait(side, y_, j):
        ref = wbuf.at[b_rows(side, y_, j)]
        remote(ref, ref, b_send.at[0], b_recv.at[side, y_, j], dev_xp).wait_recv()

    def b_forward(side, j, n):
        @pl.when(j % 2 == 0)
        def _():
            b_copy(side, y_dn, j, n, dev_yu, side).start()

        @pl.when(j % 2 == 1)
        def _():
            b_copy(side, y_up, j, n, dev_yd, side).start()

    def project(side, y_, first=False):
        base = (((xl + side) % 2) * 4 + y_) * 1024
        for n in range(2):
            cols = pl.ds(pl.multiple_of(base + n * 512, 512), 512)
            part = jnp.dot(hid[:, cols], wbuf[cols, :], preferred_element_type=jnp.float32)
            if first and n == 0:
                acc[...] = part
            else:
                acc[...] += part

    @pl.when(source)
    def _():
        pltpu.make_async_copy(send_o, wobuf.at[half_rows], sib_sem.at[0]).wait()
        remote(send_o, wobuf.at[half_rows], sib_sem.at[1], sib_sem.at[2], dev_sib).wait_recv()

        @pl.loop(0, O_EARLY)
        def _(k):
            o_copy(0, slot, k, 4 * k, dev_yu, 0).start()
            o_copy(0, slot, k, 4 * k + 1, dev_yd, 0).start()

    @pl.loop(0, Q_CHUNKS)
    def _(j):
        @pl.loop(0, 2)
        def _(n):
            src_t = b_chip(j) * 2 + n
            rows = pl.ds(pl.multiple_of(dp * 1024 + src_t * 64, 64), 64)
            ref = wbuf.at[rows]
            remote(ref, ref, a_send.at[0], a_recv.at[src_t], dev_xp).wait_recv()

        b_copy(0, y, j, 3 * j, dev_xp, 1).start()
        b_copy(0, y, j, 3 * j + 1, dev_yu, 0).start()
        b_copy(0, y, j, 3 * j + 2, dev_yd, 0).start()

    @pl.loop(0, Q_FIRST)
    def _(j):
        n = 24 + 4 * j
        b_wait(1, y, j)
        b_copy(1, y, j, n, dev_yu, 1).start()
        b_copy(1, y, j, n + 1, dev_yd, 1).start()
        b_wait(0, y_dn, j)
        b_wait(0, y_up, j)
        b_forward(0, j, n + 2)

    @pl.loop(Q_FIRST, Q_CHUNKS)
    def _(j):
        n = 24 + 4 * j
        b_wait(0, y_dn, j)
        b_copy(0, y_dn, j, n, dev_xp, 1).start()
        b_wait(0, y_up, j)
        b_copy(0, y_up, j, n + 1, dev_xp, 1).start()
        b_forward(0, j, n + 2)

    @pl.loop(0, Q_FIRST)
    def _(j):
        b_wait(1, y_dn, j)
        b_wait(1, y_up, j)
        b_forward(1, j, 24 + 4 * j + 3)

    project(0, y, first=True)

    @pl.loop(Q_FIRST, Q_CHUNKS)
    def _(j):
        b_wait(0, y_op, j)
        b_copy(0, y_op, j, 24 + 4 * j + 3, dev_xp, 1).start()

    @pl.when(source)
    def _():
        @pl.loop(0, O_FIRST)
        def _(k):
            o_copy(0, slot, k, 4 * k + 2, dev_xp, 1).start()

    @pl.when(source)
    def _():
        @pl.loop(O_EARLY, O_CHUNKS)
        def _(k):
            o_copy(0, slot, k, 4 * k, dev_yu, 0).start()
            o_copy(0, slot, k, 4 * k + 1, dev_yd, 0).start()

    def o_pass(k):
        o_wait(0, s_dn, k)
        o_wait(0, s_up, k)

        @pl.when(k >= O_FIRST)
        def _():
            o_copy(0, s_dn, k, 4 * k + 1, dev_xp, 1).start()
            o_copy(0, s_up, k, 4 * k + 2, dev_xp, 1).start()

        o_forward(0, k, 4 * k)

    @pl.when(jnp.logical_not(source))
    def _():
        @pl.loop(0, O_EARLY)
        def _(k):
            o_pass(k)

    project(0, y_dn)
    project(0, y_up)

    @pl.loop(0, Q_FIRST)
    def _(j):
        b_wait(0, y_op, j)

    project(0, y_op)

    @pl.loop(Q_FIRST, Q_CHUNKS)
    def _(j):
        b_wait(1, y, j)

    project(1, y)

    @pl.loop(0, 2)
    def _(n):
        y_ = jnp.where(n == 0, y_dn, y_up)

        @pl.loop(Q_FIRST, Q_CHUNKS)
        def _(j):
            b_wait(1, y_, j)

        project(1, y_)

    @pl.loop(0, Q_CHUNKS)
    def _(j):
        b_wait(1, y_op, j)

    project(1, y_op)

    g_me = group_of(t)

    def rotated(x):
        return x * cos[...] + pltpu.roll(x, 64, 1) * sin[...]

    bias_kv = jnp.where(c == 0, bk[pl.ds(g_me // 2, 1), :], bv[pl.ds(g_me // 2, 1), :])
    raw = acc[:, 512:640] + bias_kv
    kv_own[...] = jnp.where(c == 0, rotated(raw), raw).astype(jnp.bfloat16)
    kv_swap = remote(kv_own, kv_oth, kv_sem.at[0], kv_sem.at[1], dev_kv)
    kv_swap.start()

    @pl.when(source)
    def _():
        @pl.loop(O_FIRST, O_CHUNKS)
        def _(k):
            o_copy(0, slot, k, 4 * k + 2, dev_xp, 1).start()

    @pl.when(jnp.logical_not(source))
    def _():
        @pl.loop(O_EARLY, O_MID)
        def _(k):
            o_pass(k)

    for h in range(4):
        cols = slice(h * 128, (h + 1) * 128)
        raw_q = acc[:, cols] + bq[pl.ds(g_me * 4 + h, 1), :]
        qb[:, cols] = rotated(raw_q).astype(jnp.bfloat16)

    kv_swap.wait()
    keys = jnp.where(c == 0, kv_own[...], kv_oth[...])
    values = jnp.where(c == 0, kv_oth[...], kv_own[...])
    kv_own[...] = keys
    kv_oth[...] = values

    def t_ref(src_t, h):
        return att.at[group_of(src_t), pl.ds(pl.multiple_of(h * T_ROWS, T_ROWS), T_ROWS)]

    def t_copy(src_t, h, n, device):
        ref = t_ref(src_t, h)
        return remote(ref, ref, t_send.at[n], t_recv.at[src_t, h], device)

    def t_wait(src_t, h):
        ref = t_ref(src_t, h)
        remote(ref, ref, t_send.at[0], t_recv.at[src_t, h], dev_sib).wait_recv()

    def tid(xh_, z_, c_):
        return xh_ * 8 + z_ * 2 + c_

    def gather_cross(copy, wait, chunks, first):
        own = tid(1 - xh, z, c)

        @pl.loop(0, chunks)
        def _(h):
            wait(own, h)

            @pl.when(h < first)
            def _():
                copy(own, h, 15 * h + 8, dev_zu).start()
                copy(own, h, 15 * h + 9, dev_zd).start()

            copy(own, h, 15 * h + 10, dev_sib).start()

    def gather_side(copy, wait, chunks, first, side):
        xs = (xh + side) % 2
        dn, up = tid(xs, z_dn, c), tid(xs, z_up, c)
        @pl.loop(0, chunks)
        def _(h):
            n = 15 * h + 4 + 7 * side
            wait(dn, h)
            wait(up, h)
            along = h < first if side == 1 else h >= 0

            @pl.when(jnp.logical_and(along, h % 2 == 0))
            def _():
                copy(dn, h, n, dev_zu).start()

            @pl.when(jnp.logical_and(along, h % 2 == 1))
            def _():
                copy(up, h, n, dev_zd).start()

            if side == 0:

                @pl.when(h >= first)
                def _():
                    copy(dn, h, 15 * h + 8, dev_xh).start()
                    copy(up, h, 15 * h + 9, dev_xh).start()

            copy(dn, h, n + 1, dev_sib).start()
            copy(up, h, n + 2, dev_sib).start()

    def gather_last(copy, wait, chunks, first, side):
        @pl.loop(0, chunks)
        def _(h):
            op = tid((xh + side) % 2, z_op, c)
            wait(op, h)
            if side == 0:

                @pl.when(h >= first)
                def _():
                    copy(op, h, 15 * h + 11, dev_xh).start()

            copy(op, h, 15 * h + 7 + 7 * side, dev_sib).start()

    def start_own(copy, h):
        copy(t, h, 15 * h, dev_xh).start()
        copy(t, h, 15 * h + 1, dev_zu).start()
        copy(t, h, 15 * h + 2, dev_zd).start()
        copy(t, h, 15 * h + 3, dev_sib).start()

    def wait_sibling(wait, chunks):
        @pl.loop(0, 8)
        def _(n):
            @pl.loop(0, chunks)
            def _(h):
                wait(n * 2 + 1 - c, h)

    length = len_ref[0]

    for n in range(2):
        lo, hi = n * 256, (n + 1) * 256

        @pl.loop(0, 4)
        def _(h):
            cols = pl.ds(pl.multiple_of(h * 128, 128), 128)
            s = lax.dot_general(
                qb[lo:hi, cols], kv_own[0:hi, :], (((1,), (1,)), ((), ())), preferred_element_type=jnp.float32
            ) * HD ** (-0.5)
            r = lax.broadcasted_iota(jnp.int32, (256, hi), 0) + lo
            k = lax.broadcasted_iota(jnp.int32, (256, hi), 1)
            s = jnp.where((k <= r) & (k < length), s, -1e30)
            e = jnp.exp(s - jnp.max(s, axis=1, keepdims=True))
            p = (e / jnp.sum(e, axis=1, keepdims=True)).astype(jnp.bfloat16)
            o = jnp.dot(p, kv_oth[0:hi, :], preferred_element_type=jnp.float32)
            att[g_me, lo:hi, cols] = o.astype(jnp.bfloat16)

        start_own(t_copy, 2 * n)
        start_own(t_copy, 2 * n + 1)

    @pl.when(source)
    def _():
        @pl.loop(0, O_FIRST)
        def _(k):
            o_wait(1, slot, k)
            o_copy(1, slot, k, 4 * O_CHUNKS + 2 * k, dev_yu, 1).start()
            o_copy(1, slot, k, 4 * O_CHUNKS + 2 * k + 1, dev_yd, 1).start()

    @pl.when(jnp.logical_not(source))
    def _():
        @pl.loop(O_MID, O_CHUNKS)
        def _(k):
            o_wait(0, s_dn, k)
            o_wait(0, s_up, k)
            o_forward(0, k, 4 * k)

    gather_side(t_copy, t_wait, T_CHUNKS, T_CHUNKS, 0)
    gather_cross(t_copy, t_wait, T_CHUNKS, T_CHUNKS)

    @pl.when(source)
    def _():
        @pl.loop(0, O_CHUNKS)
        def _(k):
            o_wait(0, 1 - slot, k)

            @pl.when(k >= O_FIRST)
            def _():
                o_copy(0, 1 - slot, k, 4 * k + 3, dev_xp, 1).start()

    @pl.when(jnp.logical_not(source))
    def _():
        @pl.loop(O_MID, O_CHUNKS)
        def _(k):
            o_copy(0, s_dn, k, 4 * k + 1, dev_xp, 1).start()
            o_copy(0, s_up, k, 4 * k + 2, dev_xp, 1).start()

    @pl.when(jnp.logical_not(source))
    def _():
        @pl.loop(0, O_FIRST)
        def _(k):
            o_wait(1, s_dn, k)
            o_wait(1, s_up, k)
            o_forward(1, k, 4 * k + 1)

    gather_side(t_copy, t_wait, T_CHUNKS, T_CHUNKS, 1)
    gather_last(t_copy, t_wait, T_CHUNKS, T_CHUNKS, 0)

    def out_block(src_t, j):
        xh_s, z_s, c_s = src_t // 8, (src_t // 2) % 4, src_t % 2
        side, s = j // 2, j % 2
        xl_b = (xl + side) % 2
        xh_b = (xh_s + side * c_s) % 2
        return (xl_b * 4 + c_s + 2 * s) * 8 + xh_b * 4 + z_s

    def g_ref(src_t, j):
        col = out_block(src_t, j // 2) * 128
        return out.at[pl.ds(pl.multiple_of((j % 2) * 256, 256), 256), pl.ds(pl.multiple_of(col, 128), 128)]

    def g_copy_own(src_t, j, n, device):
        return remote(outb.at[j], g_ref(src_t, j), g_send.at[n], g_recv.at[src_t, j], device)

    def g_copy(src_t, j, n, device):
        ref = g_ref(src_t, j)
        return remote(ref, ref, g_send.at[n], g_recv.at[src_t, j], device)

    def g_wait(src_t, j):
        ref = g_ref(src_t, j)
        remote(ref, ref, g_send.at[0], g_recv.at[src_t, j], dev_sib).wait_recv()

    def near(i):
        return (xh + i // 4) % 2, (z + ring(i % 4)) % 4

    def sibling_wait(i):
        xs, zs = near(i)

        @pl.loop(0, T_CHUNKS)
        def _(h):
            t_wait(tid(xs, zs, 1 - c), h)

    def add_pair(i, half, first=False):
        xs, zs = near(i)
        parts = []
        for core in range(2):
            g = group_of(tid(xs, zs, core))
            parts.append(
                lax.dot_general(
                    att[g],
                    wobuf[half * 256 : (half + 1) * 256, pl.ds(pl.multiple_of(g * 512, 512), 512)],
                    (((1,), (1,)), ((), ())),
                    preferred_element_type=jnp.float32,
                )
            )
        if first:
            acc2[...] = parts[0] + parts[1]
        else:
            acc2[...] += parts[0] + parts[1]

    def send_half(half):
        for n in range(4):
            j = half * 4 + n
            rows, cols = slice((n % 2) * 256, (n % 2 + 1) * 256), slice((n // 2) * 128, (n // 2 + 1) * 128)
            outb[j] = acc2[rows, cols].astype(jnp.bfloat16)
            pltpu.make_async_copy(outb.at[j], g_ref(t, j), g_loc.at[j]).start()
            start_own(g_copy_own, j)

    sibling_wait(0)
    add_pair(0, 0, True)

    @pl.loop(1, 7)
    def _(i):
        sibling_wait(i)
        add_pair(i, 0)

    gather_last(t_copy, t_wait, T_CHUNKS, T_CHUNKS, 1)
    sibling_wait(7)
    add_pair(7, 0)
    send_half(0)

    @pl.when(source)
    def _():
        @pl.loop(O_FIRST, O_CHUNKS)
        def _(k):
            o_wait(1, slot, k)

        @pl.loop(0, O_CHUNKS)
        def _(k):
            o_wait(1, 1 - slot, k)

    @pl.when(jnp.logical_not(source))
    def _():
        @pl.loop(O_FIRST, O_CHUNKS)
        def _(k):
            o_wait(1, s_dn, k)
            o_wait(1, s_up, k)

    add_pair(0, 1, True)

    @pl.loop(1, 8)
    def _(i):
        add_pair(i, 1)

    send_half(1)
    gather_side(g_copy, g_wait, G_CHUNKS, G_FIRST, 0)
    gather_last(g_copy, g_wait, G_CHUNKS, G_FIRST, 0)
    gather_cross(g_copy, g_wait, G_CHUNKS, G_FIRST)
    gather_side(g_copy, g_wait, G_CHUNKS, G_FIRST, 1)
    gather_last(g_copy, g_wait, G_CHUNKS, G_FIRST, 1)
    wait_sibling(g_wait, G_CHUNKS)

    for j in range(G_CHUNKS):
        pltpu.make_async_copy(outb.at[j], g_ref(t, j), g_loc.at[j]).wait()

    def drain(ref, sem):
        remote(ref, ref, sem, sem, dev_sib).wait_send()

    @pl.loop(1, 16)
    def _(i):
        drain(send_a.at[0], a_send.at[(t + i) % 16])

    @pl.when(jnp.logical_not(source))
    def _():
        drain(send_o, sib_sem.at[1])

    @pl.loop(0, 56)
    def _(n):
        drain(wbuf.at[0:128], b_send.at[n])

    @pl.when(source)
    def _():
        @pl.loop(0, O_CHUNKS)
        def _(k):
            for n in range(3):
                drain(wobuf.at[0:O_ROWS], o_send.at[4 * k + n])

            @pl.when(k >= O_FIRST)
            def _():
                drain(wobuf.at[0:O_ROWS], o_send.at[4 * k + 3])

            @pl.when(k < O_FIRST)
            def _():
                drain(wobuf.at[0:O_ROWS], o_send.at[4 * O_CHUNKS + 2 * k])
                drain(wobuf.at[0:O_ROWS], o_send.at[4 * O_CHUNKS + 2 * k + 1])

    @pl.when(jnp.logical_not(source))
    def _():
        @pl.loop(0, O_CHUNKS)
        def _(k):
            drain(wobuf.at[0:O_ROWS], o_send.at[4 * k])
            drain(wobuf.at[0:O_ROWS], o_send.at[4 * k + 1])

            @pl.when(k >= O_FIRST)
            def _():
                drain(wobuf.at[0:O_ROWS], o_send.at[4 * k + 2])

    @pl.loop(0, 15 * T_CHUNKS)
    def _(n):
        drain(att.at[0, 0:T_ROWS], t_send.at[n])

    @pl.loop(0, 15 * G_CHUNKS)
    def _(n):
        drain(outb.at[0], g_send.at[n])


def local(hidden, lengths, norm_gain, w_q, w_k, w_v, w_out, b_q, b_k, b_v):
    positions = np.arange(TOK, dtype=np.float32)
    freqs = np.float32(THETA) ** (-np.arange(0, HD, 2, dtype=np.float32) / np.float32(HD))
    angles = (positions[:, None] * freqs[None, :]).astype(np.float64)
    cosine, sine = np.cos(angles), np.sin(angles)
    cos = np.concatenate((cosine, cosine), axis=1).astype(np.float32)
    sin = np.concatenate((-sine, sine), axis=1).astype(np.float32)
    anywhere = pl.BlockSpec(memory_space=pl.ANY)
    hbm = pl.BlockSpec(memory_space=pltpu.HBM)
    bf, f32 = jnp.bfloat16, jnp.float32
    dma = pltpu.SemaphoreType.DMA
    result = pl.pallas_call(
        kernel,
        out_shape=jax.ShapeDtypeStruct((TOK, D), bf),
        in_specs=[pl.BlockSpec(memory_space=pltpu.SMEM)] + [hbm] * 11,
        out_specs=anywhere,
        scratch_shapes=[
            pltpu.VMEM((1, D), f32),
            pltpu.VMEM((HQ, HD), f32),
            pltpu.VMEM((KV, HD), f32),
            pltpu.VMEM((KV, HD), f32),
            pltpu.VMEM((TOK, HD), f32),
            pltpu.VMEM((TOK, HD), f32),
            pltpu.VMEM((ROWS, 18432), f32),
            pltpu.VMEM((144, 8, 128), f32),
            pltpu.VMEM((144, 128), f32),
            pltpu.VMEM((144, 128), f32),
            pltpu.VMEM((144, 128), f32),
            pltpu.VMEM((TOK, D), bf),
            pltpu.VMEM((GROUPS, ROWS, WCOLS), bf),
            pltpu.VMEM((D, WCOLS), bf),
            pltpu.VMEM((ROWS, D), bf),
            pltpu.VMEM((512, D), bf),
            pltpu.VMEM((TOK, WCOLS), f32),
            pltpu.VMEM((TOK, GCOLS), bf),
            pltpu.VMEM((TOK, HD), bf),
            pltpu.VMEM((TOK, HD), bf),
            pltpu.VMEM((GROUPS, TOK, GCOLS), bf),
            pltpu.VMEM((TOK, 256), f32),
            pltpu.VMEM((G_CHUNKS, 256, 128), bf),
            dma((11,)),
            dma((2,)),
            dma((16,)),
            dma((16,)),
            dma((56,)),
            dma((2, 4, Q_CHUNKS)),
            dma((3,)),
            dma((4 * O_CHUNKS + 2 * O_FIRST,)),
            dma((2, 2, O_CHUNKS)),
            dma((2,)),
            dma((15 * T_CHUNKS,)),
            dma((16, T_CHUNKS)),
            dma((15 * G_CHUNKS,)),
            dma((16, G_CHUNKS)),
            dma((G_CHUNKS,)),
        ],
        compiler_params=pltpu.CompilerParams(
            collective_id=0, has_side_effects=True, vmem_limit_bytes=62 * 2**20
        ),
    )(
        lengths, hidden[0], norm_gain.reshape(1, D), w_q, w_k, w_v, w_out,
        b_q.reshape(HQ, HD), b_k.reshape(KV, HD), b_v.reshape(KV, HD), cos, sin,
    )
    return result[None]


def solution(mesh):
    rows = P(("dp", "tensor"), None)
    placed = (P("dp", None, None), P("dp"), P(), rows, rows, rows, rows, P(), P(), P())
    return jax.shard_map(
        local, mesh=mesh, in_specs=placed, out_specs=P("dp", None, None), check_vma=False
    )
```

```python
import functools

import jax
import jax.numpy as jnp
import numpy as np
from jax import lax
from jax.experimental import pallas as pl
from jax.experimental.pallas import tpu as pltpu
from jax.sharding import PartitionSpec as P

D = 8192
HQ = 64
KV = 8
HD = 128
TILE = 128
TOK = 512
GROUPS = 16
GCOLS = 512
WCOLS = 640
ROWS = 64
THETA = 1000000.0
NORM_EPS = 1e-06
PEAK_EPS = 1e-06
LEVEL_TOP = 127.0
MESH = pl.DeviceIdType.MESH
QT = 64
KT = 8
Q_CHUNKS = 8
Q_FIRST = 1
O_CHUNKS = 8
O_ROWS = 16
O_FIRST = 4
O_EARLY = 0
O_MID = 6
T_CHUNKS = 4
T_ROWS = 128
G_CHUNKS = 8
G_FIRST = 4


def kernel(
    len_ref, hid_hbm, gain_hbm, wq, wk, wv, wo, bq_hbm, bk_hbm, bv_hbm, cos_hbm, sin_hbm, out,
    gain, bq, bk, bv, cos, sin, wf, pm, pk_own, pk_oth, sc, hid, send_a, wbuf, send_o, wobuf, acc, qb, kv_own, kv_oth, att, acc2, outb,
    ld_sem, pk_sem, a_send, a_recv, b_send, b_recv, sib_sem, o_send, o_recv, kv_sem, t_send, t_recv, g_send, g_recv, g_loc,
):
    dp = lax.axis_index("dp")
    t = lax.axis_index("tensor")
    xl, y = dp // 4, dp % 4
    xh, z, c = t // 8, (t // 2) % 4, t % 2

    def dev(xl_, y_, xh_, z_, c_):
        return (xl_ * 4 + y_, xh_ * 8 + z_ * 2 + c_)

    y_up, y_dn, y_op = (y + 1) % 4, (y + 3) % 4, (y + 2) % 4
    z_up, z_dn, z_op = (z + 1) % 4, (z + 3) % 4, (z + 2) % 4
    dev_yu, dev_yd = dev(xl, y_up, xh, z, c), dev(xl, y_dn, xh, z, c)
    dev_xp = dev(1 - xl, y, (xh + c) % 2, z, c)
    dev_zu, dev_zd = dev(xl, y, xh, z_up, c), dev(xl, y, xh, z_dn, c)
    dev_xh = dev(xl, y, 1 - xh, z, c)
    dev_sib = dev(xl, y, xh, z, 1 - c)
    dev_kv = dev(xl, y, (xh + xl) % 2, z, 1 - c)

    def group_of(t_):
        return ((t_ // 8 + (t_ % 2) * xl) % 2) * 8 + t_ % 8

    def remote(src, dst, ss, rs, device):
        return pltpu.make_async_remote_copy(
            src_ref=src, dst_ref=dst, send_sem=ss, recv_sem=rs, device_id=device, device_id_type=MESH
        )

    loads = (
        pltpu.make_async_copy(wq, wf.at[:, 0:8192], ld_sem.at[0]),
        pltpu.make_async_copy(wk, wf.at[:, 8192:9216], ld_sem.at[1]),
        pltpu.make_async_copy(wv, wf.at[:, 9216:10240], ld_sem.at[2]),
        pltpu.make_async_copy(wo, wf.at[:, 10240:18432], ld_sem.at[3]),
        pltpu.make_async_copy(hid_hbm, hid, ld_sem.at[4]),
        pltpu.make_async_copy(gain_hbm, gain, ld_sem.at[5]),
        pltpu.make_async_copy(bq_hbm, bq, ld_sem.at[6]),
        pltpu.make_async_copy(bk_hbm, bk, ld_sem.at[7]),
        pltpu.make_async_copy(bv_hbm, bv, ld_sem.at[8]),
        pltpu.make_async_copy(cos_hbm, cos, ld_sem.at[9]),
        pltpu.make_async_copy(sin_hbm, sin, ld_sem.at[10]),
    )
    for cp in loads[:3]:
        cp.start()

    barrier = pltpu.get_barrier_semaphore()

    @pl.loop(1, 16)
    def _(i):
        pl.semaphore_signal(barrier, inc=1, device_id=(dp, (t + i) % 16), device_id_type=MESH)

    for peer in (dev_yu, dev_yd, dev_xp):
        pl.semaphore_signal(barrier, inc=1, device_id=peer, device_id_type=MESH)

    def peaks(lo, hi):
        @pl.loop(lo, hi, unroll=4)
        def _(j):
            tile = jnp.abs(wf[:, pl.ds(pl.multiple_of(j * 128, 128), 128)])
            pm[j] = jnp.max(tile.reshape(8, 8, 128), axis=0)

        top = jnp.max(jnp.max(pm[lo:hi], axis=1), axis=1, keepdims=True)
        pk_own[lo:hi, :] = jnp.broadcast_to(top, (hi - lo, 128))

    def swap(lo, hi, n):
        rows = pl.ds(lo, hi - lo)
        return remote(pk_own.at[rows], pk_oth.at[rows], pk_sem.at[n], pk_sem.at[n + 1], dev_sib)

    def scales(lo, hi):
        full = jnp.maximum(pk_own[lo:hi, :], pk_oth[lo:hi, :])
        sc[lo:hi, :] = ((full + PEAK_EPS) / LEVEL_TOP).astype(jnp.bfloat16).astype(jnp.float32)

    first_tiles = QT + 2 * KT
    for cp in loads[:3]:
        cp.wait()
    for cp in loads[3:]:
        cp.start()
    peaks(0, first_tiles)
    pl.semaphore_wait(barrier, 18)
    first_swap = swap(0, first_tiles, 0)
    first_swap.start()
    first_swap.wait()
    scales(0, first_tiles)

    def quantized(j):
        tile = wf[:, pl.ds(pl.multiple_of(j * 128, 128), 128)]
        s = sc[pl.ds(j, 1), :]
        return (jnp.floor(tile / s + 0.5) * s).astype(jnp.bfloat16)

    my_rows = pl.ds(pl.multiple_of(dp * 1024 + t * 64, 64), 64)

    hx = (xh + c * xl) % 2

    def ring(step):
        return jnp.where(step == 1, 3, jnp.where(step == 2, 1, jnp.where(step == 3, 2, 0)))

    @pl.loop(0, 16)
    def _(i):
        to_c = i % 2
        to = ((xh + i // 8 + to_c * xl) % 2) * 8 + ((z + 4 - ring((i // 2) % 4)) % 4) * 2 + to_c
        g = group_of(to)
        for n in range(4):
            send_a[g, :, n * 128 : (n + 1) * 128] = quantized(g * 4 + n)
        send_a[g, :, 512:640] = quantized(QT + KT * to_c + g // 2)

        @pl.when(to == t)
        def _():
            pltpu.make_async_copy(send_a.at[g], wbuf.at[my_rows], a_recv.at[t]).start()

        @pl.when(to != t)
        def _():
            remote(send_a.at[g], wbuf.at[my_rows], a_send.at[to], a_recv.at[t], (dp, to)).start()

    source = y % 2 == c
    slot = y // 2

    loads[3].wait()
    peaks(first_tiles, 144)
    second_swap = swap(first_tiles, 144, 2)
    second_swap.start()
    second_swap.wait()
    scales(first_tiles, 144)

    @pl.loop(0, 64)
    def _(j):
        send_o[:, pl.ds(pl.multiple_of(j * 128, 128), 128)] = quantized(QT + 2 * KT + j)

    half_rows = pl.ds(pl.multiple_of((y // 2) * 128 + c * 64, 64), 64)

    @pl.when(source)
    def _():
        pltpu.make_async_copy(send_o, wobuf.at[half_rows], sib_sem.at[0]).start()

    @pl.when(jnp.logical_not(source))
    def _():
        remote(send_o, wobuf.at[half_rows], sib_sem.at[1], sib_sem.at[2], dev_sib).start()

    for cp in loads[4:]:
        cp.wait()

    @pl.loop(0, 32)
    def _(i):
        rows = pl.ds(pl.multiple_of(i * 16, 16), 16)
        wide = hid[rows, :].astype(jnp.float32)
        ms = jnp.mean(wide * wide, axis=1, keepdims=True)
        hid[rows, :] = (wide * lax.rsqrt(ms + NORM_EPS) * gain[...]).astype(jnp.bfloat16)

    def o_rows(side, s, k):
        return pl.ds(pl.multiple_of(side * 256 + s * 128 + k * O_ROWS, O_ROWS), O_ROWS)

    def o_copy(side, s, k, n, device, to_side):
        return remote(
            wobuf.at[o_rows(side, s, k)], wobuf.at[o_rows(to_side, s, k)], o_send.at[n],
            o_recv.at[to_side, s, k], device,
        )

    def o_wait(side, s, k):
        ref = wobuf.at[o_rows(side, s, k)]
        remote(ref, ref, o_send.at[0], o_recv.at[side, s, k], dev_xp).wait_recv()

    s_dn, s_up = y_dn // 2, y_up // 2

    def o_forward(side, k, n):
        @pl.when(k % 2 == 0)
        def _():
            o_copy(side, s_dn, k, n, dev_yu, side).start()

        @pl.when(k % 2 == 1)
        def _():
            o_copy(side, s_up, k, n, dev_yd, side).start()

    def b_chip(j):
        return ((hx + j // 4) % 2) * 4 + (z + ring(j % 4)) % 4

    def b_rows(side, y_, j):
        return pl.ds(pl.multiple_of((((xl + side) % 2) * 4 + y_) * 1024 + b_chip(j) * 128, 128), 128)

    def b_copy(side, y_, j, n, device, to_side):
        ref = wbuf.at[b_rows(side, y_, j)]
        return remote(ref, ref, b_send.at[n], b_recv.at[to_side, y_, j], device)

    def b_wait(side, y_, j):
        ref = wbuf.at[b_rows(side, y_, j)]
        remote(ref, ref, b_send.at[0], b_recv.at[side, y_, j], dev_xp).wait_recv()

    def b_forward(side, j, n):
        @pl.when(j % 2 == 0)
        def _():
            b_copy(side, y_dn, j, n, dev_yu, side).start()

        @pl.when(j % 2 == 1)
        def _():
            b_copy(side, y_up, j, n, dev_yd, side).start()

    def project(side, y_, first=False):
        base = (((xl + side) % 2) * 4 + y_) * 1024
        for n in range(2):
            cols = pl.ds(pl.multiple_of(base + n * 512, 512), 512)
            part = jnp.dot(hid[:, cols], wbuf[cols, :], preferred_element_type=jnp.float32)
            if first and n == 0:
                acc[...] = part
            else:
                acc[...] += part

    @pl.when(source)
    def _():
        pltpu.make_async_copy(send_o, wobuf.at[half_rows], sib_sem.at[0]).wait()
        remote(send_o, wobuf.at[half_rows], sib_sem.at[1], sib_sem.at[2], dev_sib).wait_recv()

        @pl.loop(0, O_EARLY)
        def _(k):
            o_copy(0, slot, k, 4 * k, dev_yu, 0).start()
            o_copy(0, slot, k, 4 * k + 1, dev_yd, 0).start()

    @pl.loop(0, Q_CHUNKS)
    def _(j):
        @pl.loop(0, 2)
        def _(n):
            src_t = b_chip(j) * 2 + n
            rows = pl.ds(pl.multiple_of(dp * 1024 + src_t * 64, 64), 64)
            ref = wbuf.at[rows]
            remote(ref, ref, a_send.at[0], a_recv.at[src_t], dev_xp).wait_recv()

        b_copy(0, y, j, 3 * j, dev_xp, 1).start()
        b_copy(0, y, j, 3 * j + 1, dev_yu, 0).start()
        b_copy(0, y, j, 3 * j + 2, dev_yd, 0).start()

    @pl.loop(0, Q_FIRST)
    def _(j):
        n = 24 + 4 * j
        b_wait(1, y, j)
        b_copy(1, y, j, n, dev_yu, 1).start()
        b_copy(1, y, j, n + 1, dev_yd, 1).start()
        b_wait(0, y_dn, j)
        b_wait(0, y_up, j)
        b_forward(0, j, n + 2)

    @pl.loop(Q_FIRST, Q_CHUNKS)
    def _(j):
        n = 24 + 4 * j
        b_wait(0, y_dn, j)
        b_copy(0, y_dn, j, n, dev_xp, 1).start()
        b_wait(0, y_up, j)
        b_copy(0, y_up, j, n + 1, dev_xp, 1).start()
        b_forward(0, j, n + 2)

    @pl.loop(0, Q_FIRST)
    def _(j):
        b_wait(1, y_dn, j)
        b_wait(1, y_up, j)
        b_forward(1, j, 24 + 4 * j + 3)

    project(0, y, first=True)

    @pl.loop(Q_FIRST, Q_CHUNKS)
    def _(j):
        b_wait(0, y_op, j)
        b_copy(0, y_op, j, 24 + 4 * j + 3, dev_xp, 1).start()

    @pl.when(source)
    def _():
        @pl.loop(0, O_FIRST)
        def _(k):
            o_copy(0, slot, k, 4 * k + 2, dev_xp, 1).start()

    @pl.when(source)
    def _():
        @pl.loop(O_EARLY, O_CHUNKS)
        def _(k):
            o_copy(0, slot, k, 4 * k, dev_yu, 0).start()
            o_copy(0, slot, k, 4 * k + 1, dev_yd, 0).start()

    def o_pass(k):
        o_wait(0, s_dn, k)
        o_wait(0, s_up, k)

        @pl.when(k >= O_FIRST)
        def _():
            o_copy(0, s_dn, k, 4 * k + 1, dev_xp, 1).start()
            o_copy(0, s_up, k, 4 * k + 2, dev_xp, 1).start()

        o_forward(0, k, 4 * k)

    @pl.when(jnp.logical_not(source))
    def _():
        @pl.loop(0, O_EARLY)
        def _(k):
            o_pass(k)

    project(0, y_dn)
    project(0, y_up)

    @pl.loop(0, Q_FIRST)
    def _(j):
        b_wait(0, y_op, j)

    project(0, y_op)

    @pl.loop(Q_FIRST, Q_CHUNKS)
    def _(j):
        b_wait(1, y, j)

    project(1, y)

    @pl.loop(0, 2)
    def _(n):
        y_ = jnp.where(n == 0, y_dn, y_up)

        @pl.loop(Q_FIRST, Q_CHUNKS)
        def _(j):
            b_wait(1, y_, j)

        project(1, y_)

    @pl.loop(0, Q_CHUNKS)
    def _(j):
        b_wait(1, y_op, j)

    project(1, y_op)

    g_me = group_of(t)

    def rotated(x):
        return x * cos[...] + pltpu.roll(x, 64, 1) * sin[...]

    bias_kv = jnp.where(c == 0, bk[pl.ds(g_me // 2, 1), :], bv[pl.ds(g_me // 2, 1), :])
    raw = acc[:, 512:640] + bias_kv
    kv_own[...] = jnp.where(c == 0, rotated(raw), raw).astype(jnp.bfloat16)
    kv_swap = remote(kv_own, kv_oth, kv_sem.at[0], kv_sem.at[1], dev_kv)
    kv_swap.start()

    @pl.when(source)
    def _():
        @pl.loop(O_FIRST, O_CHUNKS)
        def _(k):
            o_copy(0, slot, k, 4 * k + 2, dev_xp, 1).start()

    @pl.when(jnp.logical_not(source))
    def _():
        @pl.loop(O_EARLY, O_MID)
        def _(k):
            o_pass(k)

    for h in range(4):
        cols = slice(h * 128, (h + 1) * 128)
        raw_q = acc[:, cols] + bq[pl.ds(g_me * 4 + h, 1), :]
        qb[:, cols] = rotated(raw_q).astype(jnp.bfloat16)

    kv_swap.wait()
    keys = jnp.where(c == 0, kv_own[...], kv_oth[...])
    values = jnp.where(c == 0, kv_oth[...], kv_own[...])
    kv_own[...] = keys
    kv_oth[...] = values

    def t_ref(src_t, h):
        return att.at[group_of(src_t), pl.ds(pl.multiple_of(h * T_ROWS, T_ROWS), T_ROWS)]

    def t_copy(src_t, h, n, device):
        ref = t_ref(src_t, h)
        return remote(ref, ref, t_send.at[n], t_recv.at[src_t, h], device)

    def t_wait(src_t, h):
        ref = t_ref(src_t, h)
        remote(ref, ref, t_send.at[0], t_recv.at[src_t, h], dev_sib).wait_recv()

    def tid(xh_, z_, c_):
        return xh_ * 8 + z_ * 2 + c_

    def gather_cross(copy, wait, chunks, first):
        own = tid(1 - xh, z, c)

        @pl.loop(0, chunks)
        def _(h):
            wait(own, h)

            @pl.when(h < first)
            def _():
                copy(own, h, 15 * h + 8, dev_zu).start()
                copy(own, h, 15 * h + 9, dev_zd).start()

            copy(own, h, 15 * h + 10, dev_sib).start()

    def gather_side(copy, wait, chunks, first, side):
        xs = (xh + side) % 2
        dn, up = tid(xs, z_dn, c), tid(xs, z_up, c)
        @pl.loop(0, chunks)
        def _(h):
            n = 15 * h + 4 + 7 * side
            wait(dn, h)
            wait(up, h)
            along = h < first if side == 1 else h >= 0

            @pl.when(jnp.logical_and(along, h % 2 == 0))
            def _():
                copy(dn, h, n, dev_zu).start()

            @pl.when(jnp.logical_and(along, h % 2 == 1))
            def _():
                copy(up, h, n, dev_zd).start()

            if side == 0:

                @pl.when(h >= first)
                def _():
                    copy(dn, h, 15 * h + 8, dev_xh).start()
                    copy(up, h, 15 * h + 9, dev_xh).start()

            copy(dn, h, n + 1, dev_sib).start()
            copy(up, h, n + 2, dev_sib).start()

    def gather_last(copy, wait, chunks, first, side):
        @pl.loop(0, chunks)
        def _(h):
            op = tid((xh + side) % 2, z_op, c)
            wait(op, h)
            if side == 0:

                @pl.when(h >= first)
                def _():
                    copy(op, h, 15 * h + 11, dev_xh).start()

            copy(op, h, 15 * h + 7 + 7 * side, dev_sib).start()

    def start_own(copy, h):
        copy(t, h, 15 * h, dev_xh).start()
        copy(t, h, 15 * h + 1, dev_zu).start()
        copy(t, h, 15 * h + 2, dev_zd).start()
        copy(t, h, 15 * h + 3, dev_sib).start()

    def wait_sibling(wait, chunks):
        @pl.loop(0, 8)
        def _(n):
            @pl.loop(0, chunks)
            def _(h):
                wait(n * 2 + 1 - c, h)

    length = len_ref[0]

    for n in range(2):
        lo, hi = n * 256, (n + 1) * 256

        @pl.loop(0, 4)
        def _(h):
            cols = pl.ds(pl.multiple_of(h * 128, 128), 128)
            s = lax.dot_general(
                qb[lo:hi, cols], kv_own[0:hi, :], (((1,), (1,)), ((), ())), preferred_element_type=jnp.float32
            ) * HD ** (-0.5)
            r = lax.broadcasted_iota(jnp.int32, (256, hi), 0) + lo
            k = lax.broadcasted_iota(jnp.int32, (256, hi), 1)
            s = jnp.where((k <= r) & (k < length), s, -1e30)
            e = jnp.exp(s - jnp.max(s, axis=1, keepdims=True))
            p = (e / jnp.sum(e, axis=1, keepdims=True)).astype(jnp.bfloat16)
            o = jnp.dot(p, kv_oth[0:hi, :], preferred_element_type=jnp.float32)
            att[g_me, lo:hi, cols] = o.astype(jnp.bfloat16)

        start_own(t_copy, 2 * n)
        start_own(t_copy, 2 * n + 1)

    @pl.when(source)
    def _():
        @pl.loop(0, O_FIRST)
        def _(k):
            o_wait(1, slot, k)
            o_copy(1, slot, k, 4 * O_CHUNKS + 2 * k, dev_yu, 1).start()
            o_copy(1, slot, k, 4 * O_CHUNKS + 2 * k + 1, dev_yd, 1).start()

    @pl.when(jnp.logical_not(source))
    def _():
        @pl.loop(O_MID, O_CHUNKS)
        def _(k):
            o_wait(0, s_dn, k)
            o_wait(0, s_up, k)
            o_forward(0, k, 4 * k)

    gather_side(t_copy, t_wait, T_CHUNKS, T_CHUNKS, 0)
    gather_cross(t_copy, t_wait, T_CHUNKS, T_CHUNKS)

    @pl.when(source)
    def _():
        @pl.loop(0, O_CHUNKS)
        def _(k):
            o_wait(0, 1 - slot, k)

            @pl.when(k >= O_FIRST)
            def _():
                o_copy(0, 1 - slot, k, 4 * k + 3, dev_xp, 1).start()

    @pl.when(jnp.logical_not(source))
    def _():
        @pl.loop(O_MID, O_CHUNKS)
        def _(k):
            o_copy(0, s_dn, k, 4 * k + 1, dev_xp, 1).start()
            o_copy(0, s_up, k, 4 * k + 2, dev_xp, 1).start()

    @pl.when(jnp.logical_not(source))
    def _():
        @pl.loop(0, O_FIRST)
        def _(k):
            o_wait(1, s_dn, k)
            o_wait(1, s_up, k)
            o_forward(1, k, 4 * k + 1)

    gather_side(t_copy, t_wait, T_CHUNKS, T_CHUNKS, 1)
    gather_last(t_copy, t_wait, T_CHUNKS, T_CHUNKS, 0)

    def out_block(src_t, j):
        xh_s, z_s, c_s = src_t // 8, (src_t // 2) % 4, src_t % 2
        side, s = j // 2, j % 2
        xl_b = (xl + side) % 2
        xh_b = (xh_s + side * c_s) % 2
        return (xl_b * 4 + c_s + 2 * s) * 8 + xh_b * 4 + z_s

    def g_ref(src_t, j):
        col = out_block(src_t, j // 2) * 128
        return out.at[pl.ds(pl.multiple_of((j % 2) * 256, 256), 256), pl.ds(pl.multiple_of(col, 128), 128)]

    def g_copy_own(src_t, j, n, device):
        return remote(outb.at[j], g_ref(src_t, j), g_send.at[n], g_recv.at[src_t, j], device)

    def g_copy(src_t, j, n, device):
        ref = g_ref(src_t, j)
        return remote(ref, ref, g_send.at[n], g_recv.at[src_t, j], device)

    def g_wait(src_t, j):
        ref = g_ref(src_t, j)
        remote(ref, ref, g_send.at[0], g_recv.at[src_t, j], dev_sib).wait_recv()

    def near(i):
        return (xh + i // 4) % 2, (z + ring(i % 4)) % 4

    def sibling_wait(i):
        xs, zs = near(i)

        @pl.loop(0, T_CHUNKS)
        def _(h):
            t_wait(tid(xs, zs, 1 - c), h)

    def add_pair(i, half, first=False):
        xs, zs = near(i)
        parts = []
        for core in range(2):
            g = group_of(tid(xs, zs, core))
            parts.append(
                lax.dot_general(
                    att[g],
                    wobuf[half * 256 : (half + 1) * 256, pl.ds(pl.multiple_of(g * 512, 512), 512)],
                    (((1,), (1,)), ((), ())),
                    preferred_element_type=jnp.float32,
                )
            )
        if first:
            acc2[...] = parts[0] + parts[1]
        else:
            acc2[...] += parts[0] + parts[1]

    def send_half(half):
        for n in range(4):
            j = half * 4 + n
            rows, cols = slice((n % 2) * 256, (n % 2 + 1) * 256), slice((n // 2) * 128, (n // 2 + 1) * 128)
            outb[j] = acc2[rows, cols].astype(jnp.bfloat16)
            pltpu.make_async_copy(outb.at[j], g_ref(t, j), g_loc.at[j]).start()
            start_own(g_copy_own, j)

    sibling_wait(0)
    add_pair(0, 0, True)

    @pl.loop(1, 7)
    def _(i):
        sibling_wait(i)
        add_pair(i, 0)

    gather_last(t_copy, t_wait, T_CHUNKS, T_CHUNKS, 1)
    sibling_wait(7)
    add_pair(7, 0)
    send_half(0)

    @pl.when(source)
    def _():
        @pl.loop(O_FIRST, O_CHUNKS)
        def _(k):
            o_wait(1, slot, k)

        @pl.loop(0, O_CHUNKS)
        def _(k):
            o_wait(1, 1 - slot, k)

    @pl.when(jnp.logical_not(source))
    def _():
        @pl.loop(O_FIRST, O_CHUNKS)
        def _(k):
            o_wait(1, s_dn, k)
            o_wait(1, s_up, k)

    add_pair(0, 1, True)

    @pl.loop(1, 8)
    def _(i):
        add_pair(i, 1)

    send_half(1)
    gather_side(g_copy, g_wait, G_CHUNKS, G_FIRST, 0)
    gather_last(g_copy, g_wait, G_CHUNKS, G_FIRST, 0)
    gather_cross(g_copy, g_wait, G_CHUNKS, G_FIRST)
    gather_side(g_copy, g_wait, G_CHUNKS, G_FIRST, 1)
    gather_last(g_copy, g_wait, G_CHUNKS, G_FIRST, 1)
    wait_sibling(g_wait, G_CHUNKS)

    for j in range(G_CHUNKS):
        pltpu.make_async_copy(outb.at[j], g_ref(t, j), g_loc.at[j]).wait()

    def drain(ref, sem):
        remote(ref, ref, sem, sem, dev_sib).wait_send()

    @pl.loop(1, 16)
    def _(i):
        drain(send_a.at[0], a_send.at[(t + i) % 16])

    @pl.when(jnp.logical_not(source))
    def _():
        drain(send_o, sib_sem.at[1])

    @pl.loop(0, 56)
    def _(n):
        drain(wbuf.at[0:128], b_send.at[n])

    @pl.when(source)
    def _():
        @pl.loop(0, O_CHUNKS)
        def _(k):
            for n in range(3):
                drain(wobuf.at[0:O_ROWS], o_send.at[4 * k + n])

            @pl.when(k >= O_FIRST)
            def _():
                drain(wobuf.at[0:O_ROWS], o_send.at[4 * k + 3])

            @pl.when(k < O_FIRST)
            def _():
                drain(wobuf.at[0:O_ROWS], o_send.at[4 * O_CHUNKS + 2 * k])
                drain(wobuf.at[0:O_ROWS], o_send.at[4 * O_CHUNKS + 2 * k + 1])

    @pl.when(jnp.logical_not(source))
    def _():
        @pl.loop(0, O_CHUNKS)
        def _(k):
            drain(wobuf.at[0:O_ROWS], o_send.at[4 * k])
            drain(wobuf.at[0:O_ROWS], o_send.at[4 * k + 1])

            @pl.when(k >= O_FIRST)
            def _():
                drain(wobuf.at[0:O_ROWS], o_send.at[4 * k + 2])

    @pl.loop(0, 15 * T_CHUNKS)
    def _(n):
        drain(att.at[0, 0:T_ROWS], t_send.at[n])

    @pl.loop(0, 15 * G_CHUNKS)
    def _(n):
        drain(outb.at[0], g_send.at[n])


def hand_over(src, dst, held, in_sem, out_sem):
    parts = [slice(n * 32, (n + 1) * 32) for n in range(16)]
    reads = [pltpu.make_async_copy(src.at[p], held.at[p], in_sem.at[n]) for n, p in enumerate(parts)]
    writes = [pltpu.make_async_copy(held.at[p], dst.at[p], out_sem.at[n]) for n, p in enumerate(parts)]
    for cp in reads:
        cp.start()
    for read, write in zip(reads, writes):
        read.wait()
        write.start()
    for cp in writes:
        cp.wait()


def local(hidden, lengths, norm_gain, w_q, w_k, w_v, w_out, b_q, b_k, b_v):
    positions = np.arange(TOK, dtype=np.float32)
    freqs = np.float32(THETA) ** (-np.arange(0, HD, 2, dtype=np.float32) / np.float32(HD))
    angles = (positions[:, None] * freqs[None, :]).astype(np.float64)
    cosine, sine = np.cos(angles), np.sin(angles)
    cos = np.concatenate((cosine, cosine), axis=1).astype(np.float32)
    sin = np.concatenate((-sine, sine), axis=1).astype(np.float32)
    anywhere = pl.BlockSpec(memory_space=pl.ANY)
    hbm = pl.BlockSpec(memory_space=pltpu.HBM)
    bf, f32 = jnp.bfloat16, jnp.float32
    dma = pltpu.SemaphoreType.DMA
    result = pl.pallas_call(
        kernel,
        out_shape=jax.ShapeDtypeStruct((TOK, D), bf),
        in_specs=[pl.BlockSpec(memory_space=pltpu.SMEM)] + [hbm] * 11,
        out_specs=anywhere,
        scratch_shapes=[
            pltpu.VMEM((1, D), f32),
            pltpu.VMEM((HQ, HD), f32),
            pltpu.VMEM((KV, HD), f32),
            pltpu.VMEM((KV, HD), f32),
            pltpu.VMEM((TOK, HD), f32),
            pltpu.VMEM((TOK, HD), f32),
            pltpu.VMEM((ROWS, 18432), f32),
            pltpu.VMEM((144, 8, 128), f32),
            pltpu.VMEM((144, 128), f32),
            pltpu.VMEM((144, 128), f32),
            pltpu.VMEM((144, 128), f32),
            pltpu.VMEM((TOK, D), bf),
            pltpu.VMEM((GROUPS, ROWS, WCOLS), bf),
            pltpu.VMEM((D, WCOLS), bf),
            pltpu.VMEM((ROWS, D), bf),
            pltpu.VMEM((512, D), bf),
            pltpu.VMEM((TOK, WCOLS), f32),
            pltpu.VMEM((TOK, GCOLS), bf),
            pltpu.VMEM((TOK, HD), bf),
            pltpu.VMEM((TOK, HD), bf),
            pltpu.VMEM((GROUPS, TOK, GCOLS), bf),
            pltpu.VMEM((TOK, 256), f32),
            pltpu.VMEM((G_CHUNKS, 256, 128), bf),
            dma((11,)),
            dma((4,)),
            dma((16,)),
            dma((16,)),
            dma((56,)),
            dma((2, 4, Q_CHUNKS)),
            dma((3,)),
            dma((4 * O_CHUNKS + 2 * O_FIRST,)),
            dma((2, 2, O_CHUNKS)),
            dma((2,)),
            dma((15 * T_CHUNKS,)),
            dma((16, T_CHUNKS)),
            dma((15 * G_CHUNKS,)),
            dma((16, G_CHUNKS)),
            dma((G_CHUNKS,)),
        ],
        compiler_params=pltpu.CompilerParams(
            collective_id=0, has_side_effects=True, vmem_limit_bytes=62 * 2**20
        ),
    )(
        lengths, hidden[0], norm_gain.reshape(1, D), w_q, w_k, w_v, w_out,
        b_q.reshape(HQ, HD), b_k.reshape(KV, HD), b_v.reshape(KV, HD), cos, sin,
    )
    result = pl.pallas_call(
        hand_over,
        out_shape=jax.ShapeDtypeStruct((TOK, D), bf),
        in_specs=[hbm],
        out_specs=hbm,
        scratch_shapes=[pltpu.VMEM((TOK, D), bf), dma((16,)), dma((16,))],
        compiler_params=pltpu.CompilerParams(vmem_limit_bytes=32 * 2**20),
    )(result)
    return result[None]


def solution(mesh):
    rows = P(("dp", "tensor"), None)
    placed = (P("dp", None, None), P("dp"), P(), rows, rows, rows, rows, P(), P(), P())
    return jax.shard_map(
        local, mesh=mesh, in_specs=placed, out_specs=P("dp", None, None), check_vma=False
    )
```
